512 devices in a mesh: row: 32 (over y_lo, z, core), col: 16 (over y_hi, x).
Axes of the slice: x: 4, y: 8 (y_hi: 4, y_lo: 2; y = y_hi * 2 + y_lo), z: 8, core: 2. Of those that a mesh axis runs over, the one named last changes fastest.
Arguments:
- hessenberg: float32 [16384, 2, 8192], P('row', None, 'col'), may hold values from -6 to 6, as said below
- diag_factors: float32 [32, 512, 512], P('row', 'col'), may hold values from -0.25 to 0.25
- border_factors: float32 [32, 512, 512], P('row', 'col'), may hold values from -0.25 to 0.25
- window_live: int32 [2, 32], replicated, may hold values from 0 to 1, as said below
Outputs:
- updated: float32 [16384, 2, 8192], P('row', None, 'col')
The draws below stay inside these ranges and needn't reach their ends.
Inputs may be any that keep to these rules, and one draw needn't show every extreme that they name: `hessenberg`: H is upper Hessenberg: entries more than one place below the diagonal are zero. Border windows k < 16 and the last border window of the sweep act: window_live[1, k] = 1 for those k and for k = 30.
All inputs are finite; a program needn't handle non-finite values.
Results may differ from the reference program's by a relative error of at most 0.00011.
Values sent between devices are 32-bit elements; how exact they have to be, the bound alone decides.
No kernel may reach another device: no remote copies, remote signals or barrier semaphores. Data moves between devices by JAX's collectives and lax.ppermute only.
A program may use at most 64 MiB of HBM per device.

```python
import jax
import jax.numpy as jnp
from jax import lax

W = 512
NT = 32
GRIDC = 16
TC = 2
ORDER = 16384


def draw_hessenberg(key, part):
    key = jax.random.fold_in(key, 11)
    full_shape = (ORDER, TC, GRIDC * W)
    row_ids = lax.broadcasted_iota(jnp.int32, full_shape, 0)
    slot_ids = lax.broadcasted_iota(jnp.int32, full_shape, 1)
    inner_ids = lax.broadcasted_iota(jnp.int32, full_shape, 2)
    col_ids = slot_ids * (GRIDC * W) + inner_ids
    values = jnp.clip(jax.random.normal(key, full_shape, jnp.float32), -6.0, 6.0)
    return jnp.where(row_ids <= col_ids + 1, values, 0.0).astype(jnp.float32)


def draw_window_live(key, part):
    key = jax.random.fold_in(key, 23)
    flags = jax.random.randint(key, (2, NT), 0, 2, dtype=jnp.int32)
    flags = flags.at[1, :NT // 2].set(1)
    return flags.at[1, NT - 2].set(1).astype(jnp.int32)


def levels(key, shape, shards, smallest, high):
    factor_of, own = 1.0, jax.random.fold_in(key, 6)
    for dim, shards_of in shards:
        steps = jnp.exp(jax.random.uniform(jax.random.fold_in(own, dim), (shards_of,), jnp.float32, smallest / len(shards), high / len(shards)))
        factor_of = factor_of * jnp.repeat(steps, shape[dim] // shards_of).reshape([-1 if axis == dim else 1 for axis in range(len(shape))])
    return factor_of


def scatter_about(stream_key, extent, scale, most, cuts=(), kind=jnp.bfloat16):
    drawn = scale * jax.random.normal(stream_key, extent, jnp.float32)
    if cuts:
        drawn = drawn * levels(stream_key, extent, cuts, -0.22, 0.18)
    return jnp.clip(drawn, -most, most).astype(kind)


def setup_inputs(seed: int = 0) -> dict:
    seeds = jax.random.split(jax.random.key(seed), 5)
    hessenberg = draw_hessenberg(jax.random.fold_in(seeds[4], 71), 0)
    diag_factors = scatter_about(seeds[1], (NT, W, W), W ** -0.5, 0.25, ((0, 32), (1, 16)), jnp.float32)
    border_factors = scatter_about(seeds[2], (NT, W, W), W ** -0.5, 0.25, ((0, 32), (1, 16)), jnp.float32)
    window_live = draw_window_live(jax.random.fold_in(seeds[4], 71), 0)
    return dict(hessenberg=hessenberg, diag_factors=diag_factors, border_factors=border_factors, window_live=window_live)


precise = lax.Precision.HIGHEST


def apply_window(matrix, factor, first_row, active):
    zero_index = jnp.zeros((), jnp.int32)
    positions = jnp.arange(ORDER, dtype=jnp.int32)
    row_strip = lax.dynamic_slice(matrix, (first_row, zero_index), (W, ORDER))
    turned = jnp.dot(factor.T, row_strip, precision=precise, preferred_element_type=jnp.float32)
    keep_cols = (positions >= first_row) & active
    row_strip = jnp.where(keep_cols[None, :], turned, row_strip)
    matrix = lax.dynamic_update_slice(matrix, row_strip, (first_row, zero_index))
    column = lax.dynamic_slice(matrix, (zero_index, first_row), (ORDER, W))
    rotated = jnp.dot(column, factor, precision=precise, preferred_element_type=jnp.float32)
    keep_rows = (positions < first_row + W) & active
    column = jnp.where(keep_rows[:, None], rotated, column)
    return lax.dynamic_update_slice(matrix, column, (zero_index, first_row))


def reference(hessenberg, diag_factors, border_factors, window_live):
    matrix = hessenberg.reshape(ORDER, ORDER)

    def diagonal_pass(position, matrix):
        position = position.astype(jnp.int32)
        first_row = position * W
        active = window_live[0, position] == 1
        return apply_window(matrix, diag_factors[position], first_row, active)

    matrix = lax.fori_loop(0, NT, diagonal_pass, matrix)

    def border_pass(position, matrix):
        position = position.astype(jnp.int32)
        first_row = position * W + W // 2
        active = window_live[1, position] == 1
        return apply_window(matrix, border_factors[position], first_row, active)

    matrix = lax.fori_loop(0, NT - 1, border_pass, matrix)
    return matrix.reshape(ORDER, TC, GRIDC * W)
```

```python
import jax
import jax.numpy as jnp
from jax import lax
from jax.sharding import PartitionSpec as P

GRID_ROWS, GRID_COLS = 32, 16
RING = 4


def dot(a, b):
    return jnp.dot(a, b, precision=lax.Precision.HIGH, preferred_element_type=jnp.float32)


def tdot(a, b):
    return lax.dot_general(
        a, b, (((0,), (0,)), ((), ())), precision=lax.Precision.HIGH, preferred_element_type=jnp.float32
    )


def moved(value, axis, target):
    count = lax.axis_size(axis)
    pairs = [(i, target(i)) for i in range(count)]
    return lax.ppermute(value, axis, [(i, j) for i, j in pairs if j is not None and 0 <= j < count])


def moved_on(value, pairs):
    number = [(r * GRID_COLS + c, t * GRID_COLS + d) for (r, c), (t, d) in pairs]
    return lax.ppermute(value, ("row", "col"), number)


def everywhere(test, target):
    return [
        ((r, c), target(r, c)) for r in range(GRID_ROWS) for c in range(GRID_COLS) if test(r, c)
    ]


def ring_gather(piece, shifted, place):
    size = piece.shape[0]
    half = size // 2
    behind = moved(piece, "col", shifted(1))
    ahead = moved(piece, "col", shifted(-1))
    far_a = moved(behind[:half], "col", shifted(1))
    far_b = moved(ahead[half:], "col", shifted(-1))
    around = jnp.concatenate([far_a, far_b, behind, piece, ahead], 0)
    return jnp.roll(around.reshape(RING, size, -1), place - 2, axis=0)


def shards(hessenberg, diag_factors, border_factors, window_live):
    window = hessenberg.shape[0]
    half = window // 2
    row = lax.axis_index("row")
    col = lax.axis_index("col")
    last = 2 * GRID_COLS - 1
    live_d = window_live[0]
    live_b = window_live[1] * (jnp.arange(2 * GRID_COLS) < last)
    tiles = [col, col + GRID_COLS]

    def at(flags, index):
        inside = (index >= 0) & (index <= last)
        return inside & (lax.dynamic_index_in_dim(flags, jnp.clip(index, 0, last), 0, False) == 1)

    own = diag_factors[0]
    border = border_factors[0]
    above = moved(border[:, half:], "row", lambda r: r + 1)
    piece = jnp.concatenate([own, border[:, :half], above], 1)
    turned_piece = moved_on(
        piece, everywhere(lambda r, c: True, lambda r, c: (r // 16 * 16 + c, r % 16))
    )
    by_col = lax.all_gather(turned_piece, "row", axis=0, tiled=True)

    ring_y = ring_gather(piece, lambda s: (lambda c: (c + RING * s) % GRID_COLS), col // RING)
    ring_x = ring_gather(
        ring_y.reshape(RING * piece.shape[0], -1),
        lambda s: (lambda c: c // RING * RING + (c + s) % RING),
        col % RING,
    )
    by_row = ring_x.reshape(RING, RING, piece.shape[0], -1).transpose(1, 0, 2, 3).reshape(window, -1)
    left_d, left_b, left_a = by_row[:, :window], by_row[:, window : window + half], by_row[:, window + half :]

    slots = [hessenberg[:, 0], hessenberg[:, 1]]
    both = jnp.concatenate(slots, 1)
    turned = tdot(left_d, both)
    live_row = at(live_d, row)
    first = []
    for s in range(2):
        keep = (tiles[s] >= row) & live_row
        first.append(jnp.where(keep, turned[:, s * window : (s + 1) * window], slots[s]))
    corner_own = [f[0, window - 1] for f in first]
    packed = jnp.concatenate(first, 1)

    down = everywhere(lambda r, c: r < 31 and c + 16 >= r, lambda r, c: (r + 1, c))
    up = [(b, a) for a, b in down]
    from_above = moved_on(packed[half:], down)
    from_below = moved_on(packed[:half], up)
    own_top, own_bottom, below, corner_below = [], [], [], []
    for s in range(2):
        part = slice(s * window, (s + 1) * window)
        corner_below.append(from_below[0, (s + 1) * window - 1])
        below.append(jnp.where(tiles[s] > row, from_below[:, part], 0))
        own_top.append(jnp.where(tiles[s] >= row, first[s][:half], 0))
        own_bottom.append(first[s][half:])
    new_top = tdot(left_a, jnp.concatenate([from_above, jnp.concatenate(own_top, 1)], 0))
    new_bottom = tdot(left_b, jnp.concatenate([packed[half:], jnp.concatenate(below, 1)], 0))
    prev_active = at(live_b, row - 1)
    own_active = at(live_b, row)

    def sides(s):
        part = slice(s * window, (s + 1) * window)
        tile = tiles[s]
        top = jnp.where((tile >= row - 1) & prev_active, new_top[:, part], own_top[s])
        bottom = jnp.where((tile >= row) & own_active, new_bottom[:, part], own_bottom[s])
        for_right = jnp.concatenate([top, bottom], 0)
        for_left = jnp.concatenate(
            [jnp.where(tile >= row, top, 0), jnp.where(tile == row, own_bottom[s], bottom)], 0
        )
        unit = (jnp.arange(half) == 0).astype(jnp.float32)
        extra_top = jnp.where(prev_active, left_a[half], unit) * jnp.where(tile == row - 1, corner_own[s], 0)
        extra_bottom = left_b[half] * jnp.where((tile == row) & own_active, corner_below[s], 0)
        extra = jnp.concatenate([extra_top, extra_bottom], 0)
        return for_left, for_right, extra

    lefts, rights = [None, None], [None, None]
    prepared = [sides(s) for s in range(2)]
    for s in (1, 0):
        for_left, for_right, extra = prepared[s]
        factor = by_col[s * window : (s + 1) * window]
        live = at(live_d, tiles[s])
        left = jnp.where(live, dot(for_left, factor[:, :half]), for_left[:, :half])
        right = jnp.where(live, dot(for_right, factor[:, half:window]), for_right[:, half:])
        last_col = (jnp.arange(half) == half - 1).astype(jnp.float32)
        lefts[s] = left
        rights[s] = right + extra[:, None] * last_col[None, :]

    reach = lambda s: (lambda r, c: r <= c + 16 * s + 1)
    right_1 = moved_on(rights[1], [p for p in everywhere(reach(1), lambda r, c: (r, c + 1)) if p[1][1] < 16])
    left_1 = moved_on(lefts[1], everywhere(lambda r, c: r <= c + 16, lambda r, c: (r, (c - 1) % 16)))
    right_0 = moved_on(rights[0], everywhere(reach(0), lambda r, c: (r, (c + 1) % 16)))
    left_0 = moved_on(lefts[0], [p for p in everywhere(lambda r, c: r <= c, lambda r, c: (r, c - 1)) if p[1][1] >= 0])
    from_left = [right_0, jnp.where(col == 0, right_0, right_1)]
    from_right = [jnp.where(col == GRID_COLS - 1, left_1, left_0), left_1]
    top_rows = (jnp.arange(window) < half)[:, None]
    outs = []
    for s in range(2):
        tile = tiles[s]
        factor = by_col[s * window : (s + 1) * window]
        new_left = dot(jnp.concatenate([from_left[s], lefts[s]], 1), factor[:, window + half :])
        new_right = dot(jnp.concatenate([rights[s], from_right[s]], 1), factor[:, window : window + half])
        keep_left = ((row < tile) | ((row == tile) & top_rows)) & at(live_b, tile - 1)
        keep_right = ((row <= tile) | ((row == tile + 1) & top_rows)) & at(live_b, tile)
        outs.append(
            jnp.concatenate(
                [jnp.where(keep_left, new_left, lefts[s]), jnp.where(keep_right, new_right, rights[s])], 1
            )
        )
    return jnp.stack(outs, 1)


def solution(mesh):
    in_specs = (P("row", None, "col"), P("row", "col", None), P("row", "col", None), P())
    out_specs = P("row", None, "col")
    return jax.shard_map(shards, mesh=mesh, in_specs=in_specs, out_specs=out_specs, check_vma=False)
```

```python
import functools

import jax
import jax.numpy as jnp
from jax import lax
from jax.experimental import pallas as pl
from jax.experimental.pallas import tpu as pltpu
from jax.sharding import PartitionSpec as P

GRID_ROWS, GRID_COLS = 32, 16
RING = 4
W = 512
HALF = 256
LAST = 31
BF16, F32 = jnp.bfloat16, jnp.float32
PARAMS = pltpu.CompilerParams(vmem_limit_bytes=28 * 1024 * 1024)
VMEM = pl.BlockSpec(memory_space=pltpu.VMEM)
SMEM = pl.BlockSpec(memory_space=pltpu.SMEM)


def split(x):
    high = x.astype(BF16)
    return high, (x - high.astype(F32)).astype(BF16)


def product(a, b, contract):
    dims = (contract, ((), ()))
    one = lambda x, y: lax.dot_general(x, y, dims, preferred_element_type=F32)
    return one(a[0], b[0]) + (one(a[0], b[1]) + one(a[1], b[0]))


def live(ref, kind, index):
    inside = (index >= 0) & (index <= LAST - kind)
    return inside & (ref[kind, jnp.clip(index, 0, LAST)] == 1)


def moved(value, axis, target):
    count = lax.axis_size(axis)
    pairs = [(i, target(i)) for i in range(count)]
    return lax.ppermute(value, axis, [(i, j) for i, j in pairs if 0 <= j < count])


def moved_on(value, pairs):
    return lax.ppermute(
        value, ("row", "col"), [(r * GRID_COLS + c, t * GRID_COLS + d) for (r, c), (t, d) in pairs]
    )


def everywhere(test, target):
    return [((r, c), target(r, c)) for r in range(GRID_ROWS) for c in range(GRID_COLS) if test(r, c)]


def swapped(value, pairs):
    return moved_on(value, pairs + [(b, a) for a, b in pairs])


def joined(far_a, far_b, behind, own, ahead, out):
    for index, part in enumerate((far_a, far_b)):
        out[index * 16 : index * 16 + 16] = part[...]
    for index, part in enumerate((behind, own, ahead)):
        out[32 * index + 32 : 32 * index + 64] = part[...]


def left_kernel(where, lives, own, behind, ahead, far_a, far_b, h0, h1, send_a, send_b, fb_high, fb_low, d_high, d_low):
    row, col = where[0], where[1]
    ring_y, ring_x = col // RING, col % RING

    def place(ref, rows, x_off, y_offs):
        for index, y_off in enumerate(y_offs):
            at_y = lax.rem(ring_y + y_off + RING, RING)
            at_x = lax.rem(ring_x + x_off + RING, RING)
            start = pl.multiple_of((at_y * RING + at_x) * 32, 32)
            part = ref[rows + 32 * index : rows + 32 * index + 32, :]
            high, low = split(part)
            for side in range(2):
                lanes = slice(W + side * HALF, W + side * HALF + HALF)
                fb_high[side, pl.ds(start, 32), :] = high[:, lanes]
                fb_low[side, pl.ds(start, 32), :] = low[:, lanes]
            d_high[pl.ds(start, 32), :] = high[:, :W]
            d_low[pl.ds(start, 32), :] = low[:, :W]

    place(own, 0, 0, (-2, -1, 0, 1))
    place(behind, 0, -1, (-2, -1, 0, 1))
    place(ahead, 0, 1, (-2, -1, 0, 1))
    place(far_a, 0, 2, (-2, -1))
    place(far_b, 0, 2, (0, 1))
    odd = lax.rem(row, 2) == 1
    live_row = live(lives, 0, row)
    factor = (d_high[...], d_low[...])
    for s, h in enumerate((h0, h1)):
        lanes = slice(s * W, s * W + W)
        value = h[...]
        turned = product(factor, split(value), ((0,), (0,)))
        value = jnp.where((col + GRID_COLS * s >= row) & live_row, turned, value)
        send_a[:, lanes] = jnp.where(odd, value[:HALF], value[HALF:])
        send_b[:, lanes] = jnp.where(odd, value[HALF:], value[:HALF])


def prepare_kernel(gathered, high, low):
    value = gathered[...].reshape(high.shape[1], high.shape[2])
    high[0], low[0] = split(value)


def middle_kernel(first, where, lives, own, got, fb_high, fb_low, c_high, c_low, kept, side, edge0, edge1):
    row, col = where[0], where[1]
    odd = lax.rem(row, 2) == 1
    top = odd if first else ~odd
    top_index = top.astype(jnp.int32)
    active = live(lives, 1, jnp.where(top, row - 1, row))
    factor = (fb_high[top_index], fb_low[top_index])
    below_part = (fb_high[top_index, HALF:, :], fb_low[top_index, HALF:, :])
    odd_col = lax.rem(col, 2) == 1
    is_corner = (lax.broadcasted_iota(jnp.int32, (HALF, 128), 0) == 0) & (
        lax.broadcasted_iota(jnp.int32, (HALF, 128), 1) == 127
    )
    ends = []
    for s in range(2):
        lanes = slice(s * W, s * W + W)
        tile = col + GRID_COLS * s
        own_raw, got_raw = own[:, lanes], got[:, lanes]
        own_value = jnp.where(top & (tile < row), 0.0, own_raw)
        got_value = jnp.where(top | (tile > row), got_raw, 0.0)
        acted = active & (tile >= jnp.where(top, row - 1, row))
        upper, lower = jnp.where(top, got_value, own_value), jnp.where(top, own_value, got_value)
        rows = product(factor, split(jnp.concatenate([upper, lower], 0)), ((0,), (0,)))
        value = jnp.where(acted, rows, own_value)
        for_left = jnp.where(top, jnp.where(tile >= row, value, 0.0), jnp.where(tile == row, own_value, value))
        turns = live(lives, 0, tile)
        matrix = lambda a, b: (c_high[s, :, a:b], c_low[s, :, a:b])
        left = product(split(for_left), matrix(0, HALF), ((1,), (0,)))
        right = product(split(value), matrix(HALF, W), ((1,), (0,)))
        left = jnp.where(turns, left, for_left[:, :HALF])
        right = jnp.where(turns, right, value[:, HALF:])
        kept[2 * s] = left
        kept[2 * s + 1] = right
        has_corner = (top & (tile == row - 1)) | (~top & (tile == row) & acted)
        corner = jnp.where(has_corner & is_corner, jnp.where(top, own_raw[:, W - 128 :], got_raw[:, W - 128 :]), 0.0)
        spread = jnp.where(acted, product(below_part, split(corner), ((0,), (0,))), corner)
        kept[2 * s + 1, :, HALF - 128 :] = kept[2 * s + 1, :, HALF - 128 :] + spread
        right = kept[2 * s + 1]
        side[s] = jnp.where(odd_col, left, right)
        ends.append((left, right))
    crosses = col == 0
    edge0[...] = jnp.where(odd_col, ends[0][1], jnp.where(crosses, ends[1][0], ends[0][0]))
    edge1[...] = jnp.where(odd_col, ends[1][1], ends[1][0])


def last_kernel(first, where, lives, kept, side, edge0, edge1, c_high, c_low, *rest):
    out = rest[-1]
    row, col = where[0], where[1]
    odd = lax.rem(row, 2) == 1
    top = odd if first else ~odd
    odd_col = lax.rem(col, 2) == 1
    for s in range(2):
        tile = col + GRID_COLS * s
        left, right = kept[2 * s], kept[2 * s + 1]
        near = side[s]
        far = (edge0 if s == 0 else edge1)[...]
        if s == 1:
            far = jnp.where(col == 0, edge0[...], far)
        pairs = (
            (jnp.where(odd_col, near, far), left, W + HALF, live(lives, 1, tile - 1) & ((row < tile) | ((row == tile) & top))),
            (right, jnp.where(odd_col, far, near), W, live(lives, 1, tile) & ((row <= tile) | ((row == tile + 1) & top))),
        )
        for index, (one, two, at, keep) in enumerate(pairs):
            factor = (c_high[s, :, at : at + HALF], c_low[s, :, at : at + HALF])
            value = product(split(jnp.concatenate([one, two], 1)), factor, ((1,), (0,)))
            value = jnp.where(keep, value, two if index == 0 else one)
            out[:, s, index * HALF : index * HALF + HALF] = value


def shards(hessenberg, diag_factors, border_factors, window_live):
    row = lax.axis_index("row")
    col = lax.axis_index("col")
    where = jnp.stack([row, col]).astype(jnp.int32)
    shape = jax.ShapeDtypeStruct

    border = border_factors[0]
    above = moved(border[:, HALF:], "row", lambda r: r + 1)
    piece = jnp.concatenate([diag_factors[0], border[:, :HALF], above], 1)

    mine = moved_on(piece, everywhere(lambda r, c: True, lambda r, c: (r // 16 * 16 + c, r % 16)))
    other = moved_on(piece, everywhere(lambda r, c: True, lambda r, c: (16 - r // 16 * 16 + c, r % 16)))
    lower = row >= 16
    both = jnp.concatenate([jnp.where(lower, other, mine), jnp.where(lower, mine, other)], 0)
    groups = [list(range(16)), list(range(16, 32))]
    gathered = lax.all_gather(both, "row", axis=0, tiled=True, axis_index_groups=groups)
    gathered = gathered.reshape(16, 2, 32, 2 * W)

    along_y = lambda s: (lambda c: (c + RING * s) % GRID_COLS)
    along_x = lambda s: (lambda c: c // RING * RING + (c + s) % RING)
    behind = moved(piece, "col", along_y(1))
    ahead = moved(piece, "col", along_y(-1))
    far_a = moved(behind[:16], "col", along_y(1))
    far_b = moved(ahead[16:], "col", along_y(-1))
    block = pl.pallas_call(
        joined, out_shape=shape((128, 2 * W), F32), in_specs=[VMEM] * 5, out_specs=VMEM, name="joined"
    )(far_a, far_b, behind, piece, ahead)
    behind = moved(block, "col", along_x(1))
    ahead = moved(block, "col", along_x(-1))
    far_a = moved(behind[:64], "col", along_x(1))
    far_b = moved(ahead[64:], "col", along_x(-1))

    send_a, send_b, fb_high, fb_low = pl.pallas_call(
        left_kernel,
        out_shape=[shape((HALF, 2 * W), F32)] * 2 + [shape((2, W, HALF), BF16)] * 2,
        in_specs=[SMEM, SMEM] + [VMEM] * 7,
        out_specs=[VMEM] * 4,
        scratch_shapes=[pltpu.VMEM((W, W), BF16)] * 2,
        compiler_params=PARAMS,
        name="left",
    )(where, window_live, block, behind, ahead, far_a, far_b, hessenberg[:, 0], hessenberg[:, 1])

    every_col = range(GRID_COLS)
    got_b = swapped(send_b, [((r, c), (r + 1, c)) for r in range(1, 31, 2) for c in every_col])
    got_a = swapped(send_a, [((r, c), (r + 1, c)) for r in range(0, 32, 2) for c in every_col])

    c_high, c_low = pl.pallas_call(
        prepare_kernel,
        grid=(2,),
        out_shape=[shape((2, W, 2 * W), BF16)] * 2,
        in_specs=[pl.BlockSpec((16, 1, 32, 2 * W), lambda s: (0, s, 0, 0))],
        out_specs=[pl.BlockSpec((1, W, 2 * W), lambda s: (s, 0, 0))] * 2,
        compiler_params=PARAMS,
        name="prepare",
    )(gathered)

    def middle(first, own, got):
        return pl.pallas_call(
            functools.partial(middle_kernel, first),
            out_shape=[shape((4, HALF, HALF), F32), shape((2, HALF, HALF), F32)] + [shape((HALF, HALF), F32)] * 2,
            in_specs=[SMEM, SMEM] + [VMEM] * 6,
            out_specs=[VMEM] * 4,
            compiler_params=PARAMS,
            name="middle",
        )(where, window_live, own, got, fb_high, fb_low, c_high, c_low)

    def exchanged(side, edge0, edge1):
        rows = range(GRID_ROWS)
        edge1 = swapped(edge1, [((r, c), (r, c + 1)) for r in rows for c in range(1, 15, 2) if r <= c + 17])
        edge0 = swapped(edge0, [((r, c), (r, (c + 1) % 16)) for r in rows for c in range(1, 16, 2) if r <= c + 1])
        side = swapped(side, [((r, c), (r, c + 1)) for r in rows for c in range(0, 16, 2) if r <= c + 17])
        return side, edge0, edge1

    def last(first, kept, moved_parts, *done):
        place = lambda i, where: (lax.rem(where[0], 2) ^ (1 if first else 0), 0, 0)
        whole = lambda shape: pl.BlockSpec(shape, lambda i, where: (0,) * len(shape))
        lives = pl.BlockSpec(memory_space=pltpu.SMEM)
        specs = [
            lives,
            whole((4, HALF, HALF)),
            whole((2, HALF, HALF)),
            whole((HALF, HALF)),
            whole((HALF, HALF)),
            whole((2, W, 2 * W)),
            whole((2, W, 2 * W)),
        ]
        return pl.pallas_call(
            functools.partial(last_kernel, first),
            out_shape=shape((W, 2, W), F32),
            grid_spec=pltpu.PrefetchScalarGridSpec(
                num_scalar_prefetch=1,
                grid=(1,),
                in_specs=specs + [pl.BlockSpec(memory_space=pl.ANY)] * len(done),
                out_specs=pl.BlockSpec((HALF, 2, W), place),
            ),
            input_output_aliases={8: 0} if done else {},
            compiler_params=PARAMS,
            name="last",
        )(where, window_live, kept, *moved_parts, c_high, c_low, *done)

    kept_a, *ends_a = middle(True, send_a, got_a)
    parts_a = exchanged(*ends_a)
    kept_b, *ends_b = middle(False, send_b, got_b)
    parts_b = exchanged(*ends_b)
    out = last(True, kept_a, parts_a)
    return last(False, kept_b, parts_b, out)


def solution(mesh):
    in_specs = (P("row", None, "col"), P("row", "col", None), P("row", "col", None), P())
    out_specs = P("row", None, "col")
    return jax.shard_map(shards, mesh=mesh, in_specs=in_specs, out_specs=out_specs, check_vma=False)
```

```python
import functools

import jax
import jax.numpy as jnp
from jax import lax
from jax.experimental import pallas as pl
from jax.experimental.pallas import tpu as pltpu
from jax.sharding import PartitionSpec as P

GRID_ROWS, GRID_COLS = 32, 16
RING = 4
W = 512
HALF = 256
LAST = 31
BF16, F32 = jnp.bfloat16, jnp.float32
PARAMS = pltpu.CompilerParams(vmem_limit_bytes=16 * 1024 * 1024)
VMEM = pl.BlockSpec(memory_space=pltpu.VMEM)
SMEM = pl.BlockSpec(memory_space=pltpu.SMEM)


def split(x):
    high = x.astype(BF16)
    return high, (x - high.astype(F32)).astype(BF16)


def product(a, b, contract):
    dims = (contract, ((), ()))
    one = lambda x, y: lax.dot_general(x, y, dims, preferred_element_type=F32)
    return one(a[0], b[0]) + (one(a[0], b[1]) + one(a[1], b[0]))


def cost(products, megabytes):
    flops = int(products * 3 * 2 * HALF * W * 2 * W)
    return pl.CostEstimate(flops=flops, bytes_accessed=megabytes << 20, transcendentals=0)


def live(ref, kind, index):
    inside = (index >= 0) & (index <= LAST - kind)
    return inside & (ref[kind, jnp.clip(index, 0, LAST)] == 1)


def moved(value, axis, target):
    count = lax.axis_size(axis)
    pairs = [(i, target(i)) for i in range(count)]
    return lax.ppermute(value, axis, [(i, j) for i, j in pairs if 0 <= j < count])


def moved_on(value, pairs):
    return lax.ppermute(
        value, ("row", "col"), [(r * GRID_COLS + c, t * GRID_COLS + d) for (r, c), (t, d) in pairs]
    )


def everywhere(test, target):
    return [((r, c), target(r, c)) for r in range(GRID_ROWS) for c in range(GRID_COLS) if test(r, c)]


def swapped(value, pairs):
    return moved_on(value, pairs + [(b, a) for a, b in pairs])


def left_kernel(where, lives, pieces, h0, h1, send_a, send_b, fb_high, fb_low, d_high, d_low):
    row, col = where[0], where[1]
    for at_x in range(RING):
        for at_y in range(RING):
            rows = slice((at_y * RING + at_x) * 32, (at_y * RING + at_x) * 32 + 32)
            high, low = split(pieces[at_x, at_y])
            for side in range(2):
                lanes = slice(W + side * HALF, W + side * HALF + HALF)
                fb_high[side, rows, :] = high[:, lanes]
                fb_low[side, rows, :] = low[:, lanes]
            d_high[rows, :] = high[:, :W]
            d_low[rows, :] = low[:, :W]
    odd = lax.rem(row, 2) == 1
    live_row = live(lives, 0, row)
    factor = (d_high[...], d_low[...])
    for s, h in enumerate((h0, h1)):
        lanes = slice(s * W, s * W + W)
        value = h[...]
        turned = product(factor, split(value), ((0,), (0,)))
        value = jnp.where((col + GRID_COLS * s >= row) & live_row, turned, value)
        send_a[:, lanes] = jnp.where(odd, value[:HALF], value[HALF:])
        send_b[:, lanes] = jnp.where(odd, value[HALF:], value[:HALF])


def prepare_kernel(where, gathered, high, low):
    for index in range(16):
        rows = slice(32 * index, 32 * index + 32)
        high[0, rows, :], low[0, rows, :] = split(gathered[lax.rem(where[1] + index, 16), 0])


def middle_kernel(s, where, lives, own_a, own_b, got_a, got_b, fb_high, fb_low, c_high, c_low, *rest):
    kept, side, edge = rest[-3:]
    row, col = where[0], where[1]
    lanes = slice(s * W, s * W + W)
    tile = col + GRID_COLS * s
    odd_col = lax.rem(col, 2) == 1
    is_corner = (lax.broadcasted_iota(jnp.int32, (HALF, 128), 0) == 0) & (
        lax.broadcasted_iota(jnp.int32, (HALF, 128), 1) == 127
    )
    for half, (own, got) in enumerate(((own_a, got_a), (own_b, got_b))):
        top = lax.rem(row + half, 2) == 1
        top_index = top.astype(jnp.int32)
        active = live(lives, 1, jnp.where(top, row - 1, row))
        factor = (fb_high[top_index], fb_low[top_index])
        below_part = (fb_high[top_index, HALF:, :], fb_low[top_index, HALF:, :])
        own_raw, got_raw = own[:, lanes], got[:, lanes]
        own_value = jnp.where(top & (tile < row), 0.0, own_raw)
        got_value = jnp.where(top | (tile > row), got_raw, 0.0)
        acted = active & (tile >= jnp.where(top, row - 1, row))
        upper, lower = jnp.where(top, got_value, own_value), jnp.where(top, own_value, got_value)
        rows = product(factor, split(jnp.concatenate([upper, lower], 0)), ((0,), (0,)))
        value = jnp.where(acted, rows, own_value)
        for_left = jnp.where(top, jnp.where(tile >= row, value, 0.0), jnp.where(tile == row, own_value, value))
        turns = live(lives, 0, tile)
        matrix = lambda a, b: (c_high[s, :, a:b], c_low[s, :, a:b])
        left = product(split(for_left), matrix(0, HALF), ((1,), (0,)))
        right = product(split(value), matrix(HALF, W), ((1,), (0,)))
        left = jnp.where(turns, left, for_left[:, :HALF])
        right = jnp.where(turns, right, value[:, HALF:])
        has_corner = (top & (tile == row - 1)) | (~top & (tile == row) & acted)
        corner = jnp.where(has_corner & is_corner, jnp.where(top, own_raw[:, W - 128 :], got_raw[:, W - 128 :]), 0.0)
        spread = jnp.where(acted, product(below_part, split(corner), ((0,), (0,))), corner)
        right = jnp.concatenate([right[:, : HALF - 128], right[:, HALF - 128 :] + spread], 1)
        kept[half, 0], kept[half, 1] = left, right
        inward = jnp.where(odd_col, left, right)
        if s == 0:
            side[0, half] = inward
        else:
            side[half] = inward
        outward = jnp.where(odd_col, right, left)
        if s == 0:
            outward = jnp.where(col == 0, rest[0][half, 0], outward)
            side[1, half] = rest[1][half]
        edge[half] = outward


def border_column(lives, c_high, c_low, row, col, s, half, kept, near, far, part):
    tile = col + GRID_COLS * s
    top = lax.rem(row + half, 2) == 1
    odd_col = lax.rem(col, 2) == 1
    if part == 0:
        one, two, at = jnp.where(odd_col, near, far), kept[half, 0], W + HALF
        own, last_tile = two, tile
    else:
        one, two, at = kept[half, 1], jnp.where(odd_col, far, near), W
        own, last_tile = one, tile + 1
    keep = live(lives, 1, last_tile - 1) & ((row < last_tile) | ((row == last_tile) & top))
    factor = (c_high[s, :, at : at + HALF], c_low[s, :, at : at + HALF])
    value = product(split(jnp.concatenate([one, two], 1)), factor, ((1,), (0,)))
    return jnp.where(keep, value, own)


def second_tile_kernel(where, lives, kept, side, edge, c_high, c_low, out):
    row, col = where[0], where[1]
    for half in range(2):
        for part in range(2):
            value = border_column(lives, c_high, c_low, row, col, 1, half, kept, side[1, half], edge[half], part)
            out[half, :, part * HALF : part * HALF + HALF] = value


def first_tile_kernel(where, lives, kept, kept_1, side, edge, c_high, c_low, second, out):
    row, col = where[0], where[1]
    for half in range(2):
        start = pl.multiple_of(lax.rem(row + half + 1, 2) * HALF, HALF)
        place = pl.ds(start, HALF)
        for part in range(2):
            lanes = slice(part * HALF, part * HALF + HALF)
            out[place, 0, lanes] = border_column(
                lives, c_high, c_low, row, col, 0, half, kept, side[0, half], edge[half], part
            )
        out[place, 1, :] = second[half]

        @pl.when(col == 0)
        def _():
            out[place, 1, :HALF] = border_column(
                lives, c_high, c_low, row, col, 1, half, kept_1, side[1, half], edge[half], 0
            )


def shards(hessenberg, diag_factors, border_factors, window_live):
    row = lax.axis_index("row")
    col = lax.axis_index("col")
    where = jnp.stack([row, col]).astype(jnp.int32)
    shape = jax.ShapeDtypeStruct

    border = border_factors[0]
    above = moved(border[:, HALF:], "row", lambda r: r + 1)
    piece = jnp.concatenate([diag_factors[0], border[:, :HALF], above], 1)

    mine = moved_on(piece, everywhere(lambda r, c: True, lambda r, c: (r // 16 * 16 + (r + c) % 16, r % 16)))
    def shared(value, groups):
        every = jnp.broadcast_to(value[None], (RING, *value.shape))
        return lax.all_to_all(every, "col", 0, 0, axis_index_groups=groups)

    by_y = shared(piece, [[x + RING * y for y in range(RING)] for x in range(RING)])
    mine, by_y = lax.optimization_barrier((mine, by_y))
    other = moved(mine, "row", lambda r: r ^ 16)
    groups = [list(range(16)), list(range(16, 32))]
    gathered = lax.all_gather(jnp.concatenate([mine, other], 0), "row", axis=0, tiled=True, axis_index_groups=groups)
    gathered = gathered.reshape(16, 2, 32, 2 * W)
    by_row = shared(by_y.reshape(RING * 32, 2 * W), [[x + RING * y for x in range(RING)] for y in range(RING)])
    by_row = by_row.reshape(RING, RING, 32, 2 * W)

    send_a, send_b, fb_high, fb_low = pl.pallas_call(
        left_kernel,
        out_shape=[shape((HALF, 2 * W), F32)] * 2 + [shape((2, W, HALF), BF16)] * 2,
        in_specs=[SMEM, SMEM] + [VMEM] * 3,
        out_specs=[VMEM] * 4,
        scratch_shapes=[pltpu.VMEM((W, W), BF16)] * 2,
        compiler_params=PARAMS,
        cost_estimate=cost(2, 7),
        name="left",
    )(where, window_live, by_row, hessenberg[:, 0], hessenberg[:, 1])

    every_col = range(GRID_COLS)
    got_b = swapped(send_b, [((r, c), (r + 1, c)) for r in range(1, 31, 2) for c in every_col])
    got_a = swapped(send_a, [((r, c), (r + 1, c)) for r in range(0, 32, 2) for c in every_col])

    c_high, c_low = pl.pallas_call(
        prepare_kernel,
        out_shape=[shape((2, W, 2 * W), BF16)] * 2,
        grid_spec=pltpu.PrefetchScalarGridSpec(
            num_scalar_prefetch=1,
            grid=(2,),
            in_specs=[pl.BlockSpec((16, 1, 32, 2 * W), lambda s, where: (0, s ^ (where[0] // 16), 0, 0))],
            out_specs=[pl.BlockSpec((1, W, 2 * W), lambda s, where: (s, 0, 0))] * 2,
        ),
        compiler_params=PARAMS,
        cost_estimate=cost(0, 8),
        name="prepare",
    )(where, gathered)

    halves, quarters = shape((2, HALF, HALF), F32), shape((2, 2, HALF, HALF), F32)

    def middle(s, *other):
        return pl.pallas_call(
            functools.partial(middle_kernel, s),
            out_shape=[quarters, halves if s else quarters, halves],
            in_specs=[SMEM, SMEM] + [VMEM] * (8 + len(other)),
            out_specs=[VMEM] * 3,
            compiler_params=PARAMS,
            cost_estimate=cost(2, 4),
            name="middle",
        )(where, window_live, send_a, send_b, got_a, got_b, fb_high, fb_low, c_high, c_low, *other)

    rows = range(GRID_ROWS)
    kept_1, side_1, edge_1 = middle(1)
    edge_1 = swapped(edge_1, [((r, c), (r, c + 1)) for r in rows for c in range(1, 15, 2) if r <= c + 17])
    kept_0, sides, edge_0 = middle(0, kept_1, side_1)
    edge_0 = swapped(edge_0, [((r, c), (r, (c + 1) % 16)) for r in rows for c in range(1, 16, 2) if r <= c + 1])
    sides = swapped(sides, [((r, c), (r, c + 1)) for r in rows for c in range(0, 16, 2) if r <= c + 17])

    second = pl.pallas_call(
        second_tile_kernel,
        out_shape=shape((2, HALF, W), F32),
        in_specs=[SMEM, SMEM] + [VMEM] * 5,
        out_specs=VMEM,
        compiler_params=PARAMS,
        cost_estimate=cost(1, 4),
        name="second",
    )(where, window_live, kept_1, sides, edge_1, c_high, c_low)
    return pl.pallas_call(
        first_tile_kernel,
        out_shape=shape((W, 2, W), F32),
        in_specs=[SMEM, SMEM] + [VMEM] * 7,
        out_specs=VMEM,
        compiler_params=PARAMS,
        cost_estimate=cost(1, 4),
        name="first",
    )(where, window_live, kept_0, kept_1, sides, edge_0, c_high, c_low, second)


def solution(mesh):
    in_specs = (P("row", None, "col"), P("row", "col", None), P("row", "col", None), P())
    out_specs = P("row", None, "col")
    return jax.shard_map(shards, mesh=mesh, in_specs=in_specs, out_specs=out_specs, check_vma=False)
```

```python
import functools

import jax
import jax.numpy as jnp
from jax import lax
from jax.experimental import pallas as pl
from jax.experimental.pallas import tpu as pltpu
from jax.sharding import PartitionSpec as P

GRID_ROWS, GRID_COLS = 32, 16
RING = 4
W = 512
HALF = 256
LAST = 31
BF16, F32 = jnp.bfloat16, jnp.float32
PARAMS = pltpu.CompilerParams(vmem_limit_bytes=16 * 1024 * 1024)
VMEM = pl.BlockSpec(memory_space=pltpu.VMEM)
SMEM = pl.BlockSpec(memory_space=pltpu.SMEM)


def split(x):
    high = x.astype(BF16)
    return high, (x - high.astype(F32)).astype(BF16)


def product(a, b, contract):
    dims = (contract, ((), ()))
    one = lambda x, y: lax.dot_general(x, y, dims, preferred_element_type=F32)
    return one(a[0], b[0]) + (one(a[0], b[1]) + one(a[1], b[0]))


def cost(products, megabytes):
    flops = int(products * 3 * 2 * HALF * W * 2 * W)
    return pl.CostEstimate(flops=flops, bytes_accessed=megabytes << 20, transcendentals=0)


def live(ref, kind, index):
    inside = (index >= 0) & (index <= LAST - kind)
    return inside & (ref[kind, jnp.clip(index, 0, LAST)] == 1)


def moved(value, axis, target):
    count = lax.axis_size(axis)
    pairs = [(i, target(i)) for i in range(count)]
    return lax.ppermute(value, axis, [(i, j) for i, j in pairs if 0 <= j < count])


def moved_on(value, pairs):
    return lax.ppermute(
        value, ("row", "col"), [(r * GRID_COLS + c, t * GRID_COLS + d) for (r, c), (t, d) in pairs]
    )


def everywhere(test, target):
    return [((r, c), target(r, c)) for r in range(GRID_ROWS) for c in range(GRID_COLS) if test(r, c)]


def swapped(value, pairs):
    return moved_on(value, pairs + [(b, a) for a, b in pairs])


def in_order(pieces, x, y):
    return slice((y * RING + x) * 32, (y * RING + x) * 32 + 32), split(pieces[x, y])


def borders_kernel(pieces, fb_high, fb_low):
    for x in range(RING):
        for y in range(RING):
            rows, (high, low) = in_order(pieces, x, y)
            for side in range(2):
                lanes = slice(side * HALF, side * HALF + HALF)
                fb_high[side, rows, :] = high[:, lanes]
                fb_low[side, rows, :] = low[:, lanes]


def left_kernel(where, lives, pieces, h0, h1, send_a, send_b, d_high, d_low):
    row, col = where[0], where[1]
    for x in range(RING):
        for y in range(RING):
            rows, (high, low) = in_order(pieces, x, y)
            d_high[rows, :] = high
            d_low[rows, :] = low
    odd = lax.rem(row, 2) == 1
    live_row = live(lives, 0, row)
    factor = (d_high[...], d_low[...])
    for s, h in enumerate((h0, h1)):
        lanes = slice(s * W, s * W + W)
        value = h[...]
        turned = product(factor, split(value), ((0,), (0,)))
        value = jnp.where((col + GRID_COLS * s >= row) & live_row, turned, value)
        send_a[:, lanes] = jnp.where(odd, value[:HALF], value[HALF:])
        send_b[:, lanes] = jnp.where(odd, value[HALF:], value[:HALF])


def prepare_kernel(where, gathered, high, low):
    for index in range(16):
        rows = slice(32 * index, 32 * index + 32)
        high[0, rows, :], low[0, rows, :] = split(gathered[lax.rem(where[1] + index, 16), 0])


def middle_kernel(first, where, lives, own, got, fb_high, fb_low, c_high, c_low, kept, side, edge0, edge1):
    row, col = where[0], where[1]
    odd = lax.rem(row, 2) == 1
    top = odd if first else ~odd
    top_index = top.astype(jnp.int32)
    active = live(lives, 1, jnp.where(top, row - 1, row))
    factor = (fb_high[top_index], fb_low[top_index])
    below_part = (fb_high[top_index, HALF:, :], fb_low[top_index, HALF:, :])
    odd_col = lax.rem(col, 2) == 1
    is_corner = (lax.broadcasted_iota(jnp.int32, (HALF, 128), 0) == 0) & (
        lax.broadcasted_iota(jnp.int32, (HALF, 128), 1) == 127
    )
    ends = []
    for s in range(2):
        lanes = slice(s * W, s * W + W)
        tile = col + GRID_COLS * s
        own_raw, got_raw = own[:, lanes], got[:, lanes]
        own_value = jnp.where(top & (tile < row), 0.0, own_raw)
        got_value = jnp.where(top | (tile > row), got_raw, 0.0)
        acted = active & (tile >= jnp.where(top, row - 1, row))
        upper, lower = jnp.where(top, got_value, own_value), jnp.where(top, own_value, got_value)
        rows = product(factor, split(jnp.concatenate([upper, lower], 0)), ((0,), (0,)))
        value = jnp.where(acted, rows, own_value)
        for_left = jnp.where(top, jnp.where(tile >= row, value, 0.0), jnp.where(tile == row, own_value, value))
        turns = live(lives, 0, tile)
        matrix = lambda a, b: (c_high[s, :, a:b], c_low[s, :, a:b])
        left = product(split(for_left), matrix(0, HALF), ((1,), (0,)))
        right = product(split(value), matrix(HALF, W), ((1,), (0,)))
        left = jnp.where(turns, left, for_left[:, :HALF])
        right = jnp.where(turns, right, value[:, HALF:])
        kept[2 * s] = left
        kept[2 * s + 1] = right
        has_corner = (top & (tile == row - 1)) | (~top & (tile == row) & acted)
        corner = jnp.where(has_corner & is_corner, jnp.where(top, own_raw[:, W - 128 :], got_raw[:, W - 128 :]), 0.0)
        spread = jnp.where(acted, product(below_part, split(corner), ((0,), (0,))), corner)
        kept[2 * s + 1, :, HALF - 128 :] = kept[2 * s + 1, :, HALF - 128 :] + spread
        right = kept[2 * s + 1]
        side[s] = jnp.where(odd_col, left, right)
        ends.append((left, right))
    crosses = col == 0
    edge0[...] = jnp.where(odd_col, ends[0][1], jnp.where(crosses, ends[1][0], ends[0][0]))
    edge1[...] = jnp.where(odd_col, ends[1][1], ends[1][0])


def last_kernel(first, where, lives, kept, side, edge1, edge0, c_high, c_low, *rest):
    out = rest[-1]
    row, col = where[0], where[1]
    odd = lax.rem(row, 2) == 1
    top = odd if first else ~odd
    odd_col = lax.rem(col, 2) == 1
    for s in range(2):
        tile = col + GRID_COLS * s
        left, right = kept[2 * s], kept[2 * s + 1]
        near = side[s]
        far = (edge0 if s == 0 else edge1)[...]
        if s == 1:
            far = jnp.where(col == 0, edge0[...], far)
        pairs = (
            (jnp.where(odd_col, near, far), left, W + HALF, live(lives, 1, tile - 1) & ((row < tile) | ((row == tile) & top))),
            (right, jnp.where(odd_col, far, near), W, live(lives, 1, tile) & ((row <= tile) | ((row == tile + 1) & top))),
        )
        for index, (one, two, at, keep) in enumerate(pairs):
            factor = (c_high[s, :, at : at + HALF], c_low[s, :, at : at + HALF])
            value = product(split(jnp.concatenate([one, two], 1)), factor, ((1,), (0,)))
            value = jnp.where(keep, value, two if index == 0 else one)
            out[:, s, index * HALF : index * HALF + HALF] = value


def shards(hessenberg, diag_factors, border_factors, window_live):
    row = lax.axis_index("row")
    col = lax.axis_index("col")
    where = jnp.stack([row, col]).astype(jnp.int32)
    shape = jax.ShapeDtypeStruct

    border = border_factors[0]
    above = moved(border[:, HALF:], "row", lambda r: r + 1)
    piece = jnp.concatenate([diag_factors[0], border[:, :HALF], above], 1)

    mine = moved_on(piece, everywhere(lambda r, c: True, lambda r, c: (r // 16 * 16 + (r + c) % 16, r % 16)))
    other = moved(mine, "row", lambda r: r ^ 16)
    groups = [list(range(16)), list(range(16, 32))]
    gathered = lax.all_gather(jnp.concatenate([mine, other], 0), "row", axis=0, tiled=True, axis_index_groups=groups)
    gathered = gathered.reshape(16, 2, 32, 2 * W)

    def shared(value, groups):
        every = jnp.broadcast_to(value[None], (RING, *value.shape))
        return lax.all_to_all(every, "col", 0, 0, axis_index_groups=groups)

    by_y = shared(piece, [[x + RING * y for y in range(RING)] for x in range(RING)])
    by_y = by_y.reshape(RING * 32, 2 * W)
    along_x = [[x + RING * y for x in range(RING)] for y in range(RING)]
    diag_row = shared(by_y[:, :W], along_x).reshape(RING, RING, 32, W)
    diag_row, border_y = lax.optimization_barrier((diag_row, by_y[:, W:]))
    border_row = shared(border_y, along_x).reshape(RING, RING, 32, W)
    fb_high, fb_low = pl.pallas_call(
        borders_kernel,
        out_shape=[shape((2, W, HALF), BF16)] * 2,
        in_specs=[VMEM],
        out_specs=[VMEM] * 2,
        compiler_params=PARAMS,
        cost_estimate=cost(0, 2),
        name="borders",
    )(border_row)

    send_a, send_b = pl.pallas_call(
        left_kernel,
        out_shape=[shape((HALF, 2 * W), F32)] * 2,
        in_specs=[SMEM, SMEM] + [VMEM] * 3,
        out_specs=[VMEM] * 2,
        scratch_shapes=[pltpu.VMEM((W, W), BF16)] * 2,
        compiler_params=PARAMS,
        cost_estimate=cost(2, 7),
        name="left",
    )(where, window_live, diag_row, hessenberg[:, 0], hessenberg[:, 1])

    every_col = range(GRID_COLS)
    got_b = swapped(send_b, [((r, c), (r + 1, c)) for r in range(1, 31, 2) for c in every_col])
    got_a = swapped(send_a, [((r, c), (r + 1, c)) for r in range(0, 32, 2) for c in every_col])

    c_high, c_low = pl.pallas_call(
        prepare_kernel,
        out_shape=[shape((2, W, 2 * W), BF16)] * 2,
        grid_spec=pltpu.PrefetchScalarGridSpec(
            num_scalar_prefetch=1,
            grid=(2,),
            in_specs=[pl.BlockSpec((16, 1, 32, 2 * W), lambda s, where: (0, s ^ (where[0] // 16), 0, 0))],
            out_specs=[pl.BlockSpec((1, W, 2 * W), lambda s, where: (s, 0, 0))] * 2,
        ),
        compiler_params=PARAMS,
        cost_estimate=cost(0, 8),
        name="prepare",
    )(where, gathered)

    def middle(first, own, got):
        return pl.pallas_call(
            functools.partial(middle_kernel, first),
            out_shape=[shape((4, HALF, HALF), F32), shape((2, HALF, HALF), F32)] + [shape((HALF, HALF), F32)] * 2,
            in_specs=[SMEM, SMEM] + [VMEM] * 6,
            out_specs=[VMEM] * 4,
            compiler_params=PARAMS,
            cost_estimate=cost(2, 4),
            name="middle",
        )(where, window_live, own, got, fb_high, fb_low, c_high, c_low)

    def exchanged(side, edge0, edge1):
        rows = range(GRID_ROWS)
        side = swapped(side, [((r, c), (r, c + 1)) for r in rows for c in range(0, 16, 2) if r <= c + 17])
        edge0 = swapped(edge0, [((r, c), (r, (c + 1) % 16)) for r in rows for c in range(1, 16, 2) if r <= c + 1])
        edge1 = swapped(edge1, [((r, c), (r, c + 1)) for r in rows for c in range(1, 15, 2) if r <= c + 17])
        return side, edge1, edge0

    def last(first, kept, moved_parts, *done):
        place = lambda i, where: (lax.rem(where[0], 2) ^ (1 if first else 0), 0, 0)
        whole = lambda shape: pl.BlockSpec(shape, lambda i, where: (0,) * len(shape))
        lives = pl.BlockSpec(memory_space=pltpu.SMEM)
        specs = [
            lives,
            whole((4, HALF, HALF)),
            whole((2, HALF, HALF)),
            whole((HALF, HALF)),
            whole((HALF, HALF)),
            whole((2, W, 2 * W)),
            whole((2, W, 2 * W)),
        ]
        return pl.pallas_call(
            functools.partial(last_kernel, first),
            out_shape=shape((W, 2, W), F32),
            grid_spec=pltpu.PrefetchScalarGridSpec(
                num_scalar_prefetch=1,
                grid=(1,),
                in_specs=specs + [pl.BlockSpec(memory_space=pl.ANY)] * len(done),
                out_specs=pl.BlockSpec((HALF, 2, W), place),
            ),
            input_output_aliases={8: 0} if done else {},
            compiler_params=PARAMS,
            cost_estimate=cost(1, 4),
            name="last",
        )(where, window_live, kept, *moved_parts, c_high, c_low, *done)

    kept_a, *ends_a = middle(True, send_a, got_a)
    parts_a = exchanged(*ends_a)
    kept_b, *ends_b = middle(False, send_b, got_b)
    parts_b = exchanged(*ends_b)
    out = last(True, kept_a, parts_a)
    return last(False, kept_b, parts_b, out)


def solution(mesh):
    in_specs = (P("row", None, "col"), P("row", "col", None), P("row", "col", None), P())
    out_specs = P("row", None, "col")
    return jax.shard_map(shards, mesh=mesh, in_specs=in_specs, out_specs=out_specs, check_vma=False)
```

```python
import functools

import jax
import jax.numpy as jnp
from jax import lax
from jax.experimental import pallas as pl
from jax.experimental.pallas import tpu as pltpu
from jax.sharding import PartitionSpec as P

GRID_ROWS, GRID_COLS = 32, 16
RING = 4
W = 512
HALF = 256
LAST = 31
BF16, F32 = jnp.bfloat16, jnp.float32
PARAMS = pltpu.CompilerParams(vmem_limit_bytes=16 * 1024 * 1024)
VMEM = pl.BlockSpec(memory_space=pltpu.VMEM)
SMEM = pl.BlockSpec(memory_space=pltpu.SMEM)


def split(x):
    high = x.astype(BF16)
    return high, (x - high.astype(F32)).astype(BF16)


def product(a, b, contract):
    dims = (contract, ((), ()))
    one = lambda x, y: lax.dot_general(x, y, dims, preferred_element_type=F32)
    return one(a[0], b[0]) + (one(a[0], b[1]) + one(a[1], b[0]))


def cost(products, megabytes):
    flops = int(products * 3 * 2 * HALF * W * 2 * W)
    return pl.CostEstimate(flops=flops, bytes_accessed=megabytes << 20, transcendentals=0)


def live(ref, kind, index):
    inside = (index >= 0) & (index <= LAST - kind)
    return inside & (ref[kind, jnp.clip(index, 0, LAST)] == 1)


def moved(value, axis, target):
    count = lax.axis_size(axis)
    pairs = [(i, target(i)) for i in range(count)]
    return lax.ppermute(value, axis, [(i, j) for i, j in pairs if 0 <= j < count])


def moved_on(value, pairs):
    return lax.ppermute(
        value, ("row", "col"), [(r * GRID_COLS + c, t * GRID_COLS + d) for (r, c), (t, d) in pairs]
    )


def everywhere(test, target):
    return [((r, c), target(r, c)) for r in range(GRID_ROWS) for c in range(GRID_COLS) if test(r, c)]


def swapped(value, pairs):
    return moved_on(value, pairs + [(b, a) for a, b in pairs])


def left_kernel(where, lives, pieces, h0, h1, send_a, send_b, fb_high, fb_low, d_high, d_low):
    row, col = where[0], where[1]
    for x in range(RING):
        for y in range(RING):
            rows = slice((y * RING + x) * 32, (y * RING + x) * 32 + 32)
            high, low = split(pieces[x, y])
            for side in range(2):
                lanes = slice(W + side * HALF, W + side * HALF + HALF)
                fb_high[side, rows, :] = high[:, lanes]
                fb_low[side, rows, :] = low[:, lanes]
            d_high[rows, :] = high[:, :W]
            d_low[rows, :] = low[:, :W]
    odd = lax.rem(row, 2) == 1
    live_row = live(lives, 0, row)
    factor = (d_high[...], d_low[...])
    for s, h in enumerate((h0, h1)):
        lanes = slice(s * W, s * W + W)
        value = h[...]
        turned = product(factor, split(value), ((0,), (0,)))
        value = jnp.where((col + GRID_COLS * s >= row) & live_row, turned, value)
        send_a[:, lanes] = jnp.where(odd, value[:HALF], value[HALF:])
        send_b[:, lanes] = jnp.where(odd, value[HALF:], value[:HALF])


def prepare_kernel(where, gathered, high, low):
    for index in range(16):
        rows = slice(32 * index, 32 * index + 32)
        high[0, rows, :], low[0, rows, :] = split(gathered[lax.rem(where[1] + index, 16), 0])


def middle_kernel(first, where, lives, own, got, fb_high, fb_low, c_high, c_low, kept, side, edge0, edge1):
    row, col = where[0], where[1]
    odd = lax.rem(row, 2) == 1
    top = odd if first else ~odd
    top_index = top.astype(jnp.int32)
    active = live(lives, 1, jnp.where(top, row - 1, row))
    factor = (fb_high[top_index], fb_low[top_index])
    below_part = (fb_high[top_index, HALF:, :], fb_low[top_index, HALF:, :])
    odd_col = lax.rem(col, 2) == 1
    is_corner = (lax.broadcasted_iota(jnp.int32, (HALF, 128), 0) == 0) & (
        lax.broadcasted_iota(jnp.int32, (HALF, 128), 1) == 127
    )
    ends = []
    for s in range(2):
        lanes = slice(s * W, s * W + W)
        tile = col + GRID_COLS * s
        own_raw, got_raw = own[:, lanes], got[:, lanes]
        own_value = jnp.where(top & (tile < row), 0.0, own_raw)
        got_value = jnp.where(top | (tile > row), got_raw, 0.0)
        acted = active & (tile >= jnp.where(top, row - 1, row))
        upper, lower = jnp.where(top, got_value, own_value), jnp.where(top, own_value, got_value)
        rows = product(factor, split(jnp.concatenate([upper, lower], 0)), ((0,), (0,)))
        value = jnp.where(acted, rows, own_value)
        for_left = jnp.where(top, jnp.where(tile >= row, value, 0.0), jnp.where(tile == row, own_value, value))
        turns = live(lives, 0, tile)
        matrix = lambda a, b: (c_high[s, :, a:b], c_low[s, :, a:b])
        left = product(split(for_left), matrix(0, HALF), ((1,), (0,)))
        right = product(split(value), matrix(HALF, W), ((1,), (0,)))
        left = jnp.where(turns, left, for_left[:, :HALF])
        right = jnp.where(turns, right, value[:, HALF:])
        kept[2 * s] = left
        kept[2 * s + 1] = right
        has_corner = (top & (tile == row - 1)) | (~top & (tile == row) & acted)
        corner = jnp.where(has_corner & is_corner, jnp.where(top, own_raw[:, W - 128 :], got_raw[:, W - 128 :]), 0.0)
        spread = jnp.where(acted, product(below_part, split(corner), ((0,), (0,))), corner)
        kept[2 * s + 1, :, HALF - 128 :] = kept[2 * s + 1, :, HALF - 128 :] + spread
        right = kept[2 * s + 1]
        side[s] = jnp.where(odd_col, left, right)
        ends.append((left, right))
    crosses = col == 0
    edge0[...] = jnp.where(odd_col, ends[0][1], jnp.where(crosses, ends[1][0], ends[0][0]))
    edge1[...] = jnp.where(odd_col, ends[1][1], ends[1][0])


def last_kernel(first, where, lives, kept, side, edge1, edge0, c_high, c_low, *rest):
    out = rest[-1]
    row, col = where[0], where[1]
    odd = lax.rem(row, 2) == 1
    top = odd if first else ~odd
    odd_col = lax.rem(col, 2) == 1
    for s in range(2):
        tile = col + GRID_COLS * s
        left, right = kept[2 * s], kept[2 * s + 1]
        near = side[s]
        far = (edge0 if s == 0 else edge1)[...]
        if s == 1:
            far = jnp.where(col == 0, edge0[...], far)
        pairs = (
            (jnp.where(odd_col, near, far), left, W + HALF, live(lives, 1, tile - 1) & ((row < tile) | ((row == tile) & top))),
            (right, jnp.where(odd_col, far, near), W, live(lives, 1, tile) & ((row <= tile) | ((row == tile + 1) & top))),
        )
        for index, (one, two, at, keep) in enumerate(pairs):
            factor = (c_high[s, :, at : at + HALF], c_low[s, :, at : at + HALF])
            value = product(split(jnp.concatenate([one, two], 1)), factor, ((1,), (0,)))
            value = jnp.where(keep, value, two if index == 0 else one)
            out[:, s, index * HALF : index * HALF + HALF] = value


def shards(hessenberg, diag_factors, border_factors, window_live):
    row = lax.axis_index("row")
    col = lax.axis_index("col")
    where = jnp.stack([row, col]).astype(jnp.int32)
    shape = jax.ShapeDtypeStruct

    border = border_factors[0]
    above = moved(border[:, HALF:], "row", lambda r: r + 1)
    piece = jnp.concatenate([diag_factors[0], border[:, :HALF], above], 1)

    mine = moved_on(piece, everywhere(lambda r, c: True, lambda r, c: (r // 16 * 16 + (r + c) % 16, r % 16)))
    other = moved(mine, "row", lambda r: r ^ 16)
    groups = [list(range(16)), list(range(16, 32))]
    gathered = lax.all_gather(jnp.concatenate([mine, other], 0), "row", axis=0, tiled=True, axis_index_groups=groups)
    gathered = gathered.reshape(16, 2, 32, 2 * W)

    def shared(value, groups):
        every = jnp.broadcast_to(value[None], (RING, *value.shape))
        return lax.all_to_all(every, "col", 0, 0, axis_index_groups=groups)

    by_y = shared(piece, [[x + RING * y for y in range(RING)] for x in range(RING)])
    along_x = [[x + RING * y for x in range(RING)] for y in range(RING)]
    by_row = shared(by_y.reshape(RING * 32, 2 * W), along_x).reshape(RING, RING, 32, 2 * W)

    send_a, send_b, fb_high, fb_low = pl.pallas_call(
        left_kernel,
        out_shape=[shape((HALF, 2 * W), F32)] * 2 + [shape((2, W, HALF), BF16)] * 2,
        in_specs=[SMEM, SMEM] + [VMEM] * 3,
        out_specs=[VMEM] * 4,
        scratch_shapes=[pltpu.VMEM((W, W), BF16)] * 2,
        compiler_params=PARAMS,
        cost_estimate=cost(2, 7),
        name="left",
    )(where, window_live, by_row, hessenberg[:, 0], hessenberg[:, 1])

    every_col = range(GRID_COLS)
    got_b = swapped(send_b, [((r, c), (r + 1, c)) for r in range(1, 31, 2) for c in every_col])
    got_a = swapped(send_a, [((r, c), (r + 1, c)) for r in range(0, 32, 2) for c in every_col])

    c_high, c_low = pl.pallas_call(
        prepare_kernel,
        out_shape=[shape((2, W, 2 * W), BF16)] * 2,
        grid_spec=pltpu.PrefetchScalarGridSpec(
            num_scalar_prefetch=1,
            grid=(2,),
            in_specs=[pl.BlockSpec((16, 1, 32, 2 * W), lambda s, where: (0, s ^ (where[0] // 16), 0, 0))],
            out_specs=[pl.BlockSpec((1, W, 2 * W), lambda s, where: (s, 0, 0))] * 2,
        ),
        compiler_params=PARAMS,
        cost_estimate=cost(0, 8),
        name="prepare",
    )(where, gathered)

    def middle(first, own, got):
        return pl.pallas_call(
            functools.partial(middle_kernel, first),
            out_shape=[shape((4, HALF, HALF), F32), shape((2, HALF, HALF), F32)] + [shape((HALF, HALF), F32)] * 2,
            in_specs=[SMEM, SMEM] + [VMEM] * 6,
            out_specs=[VMEM] * 4,
            compiler_params=PARAMS,
            cost_estimate=cost(2, 4),
            name="middle",
        )(where, window_live, own, got, fb_high, fb_low, c_high, c_low)

    def exchanged(side, edge0, edge1):
        rows = range(GRID_ROWS)
        side = swapped(side, [((r, c), (r, c + 1)) for r in rows for c in range(0, 16, 2) if r <= c + 17])
        edge0 = swapped(edge0, [((r, c), (r, (c + 1) % 16)) for r in rows for c in range(1, 16, 2) if r <= c + 1])
        edge1 = swapped(edge1, [((r, c), (r, c + 1)) for r in rows for c in range(1, 15, 2) if r <= c + 17])
        return side, edge1, edge0

    def last(first, kept, moved_parts, *done):
        place = lambda i, where: (lax.rem(where[0], 2) ^ (1 if first else 0), 0, 0)
        whole = lambda shape: pl.BlockSpec(shape, lambda i, where: (0,) * len(shape))
        lives = pl.BlockSpec(memory_space=pltpu.SMEM)
        specs = [
            lives,
            whole((4, HALF, HALF)),
            whole((2, HALF, HALF)),
            whole((HALF, HALF)),
            whole((HALF, HALF)),
            whole((2, W, 2 * W)),
            whole((2, W, 2 * W)),
        ]
        return pl.pallas_call(
            functools.partial(last_kernel, first),
            out_shape=shape((W, 2, W), F32),
            grid_spec=pltpu.PrefetchScalarGridSpec(
                num_scalar_prefetch=1,
                grid=(1,),
                in_specs=specs + [pl.BlockSpec(memory_space=pl.ANY)] * len(done),
                out_specs=pl.BlockSpec((HALF, 2, W), place),
            ),
            input_output_aliases={8: 0} if done else {},
            compiler_params=PARAMS,
            cost_estimate=cost(1, 4),
            name="last",
        )(where, window_live, kept, *moved_parts, c_high, c_low, *done)

    kept_a, *ends_a = middle(True, send_a, got_a)
    parts_a = exchanged(*ends_a)
    kept_b, *ends_b = middle(False, send_b, got_b)
    parts_b = exchanged(*ends_b)
    out = last(True, kept_a, parts_a)
    return last(False, kept_b, parts_b, out)


def solution(mesh):
    in_specs = (P("row", None, "col"), P("row", "col", None), P("row", "col", None), P())
    out_specs = P("row", None, "col")
    return jax.shard_map(shards, mesh=mesh, in_specs=in_specs, out_specs=out_specs, check_vma=False)
```

```python
import functools

import jax
import jax.numpy as jnp
from jax import lax
from jax.experimental import pallas as pl
from jax.experimental.pallas import tpu as pltpu
from jax.sharding import PartitionSpec as P

GRID_ROWS, GRID_COLS = 32, 16
RING = 4
W = 512
HALF = 256
LAST = 31
BF16, F32 = jnp.bfloat16, jnp.float32
PARAMS = pltpu.CompilerParams(vmem_limit_bytes=16 * 1024 * 1024)
VMEM = pl.BlockSpec(memory_space=pltpu.VMEM)
SMEM = pl.BlockSpec(memory_space=pltpu.SMEM)


def split(x):
    high = x.astype(BF16)
    return high, (x - high.astype(F32)).astype(BF16)


def product(a, b, contract):
    dims = (contract, ((), ()))
    one = lambda x, y: lax.dot_general(x, y, dims, preferred_element_type=F32)
    return one(a[0], b[0]) + (one(a[0], b[1]) + one(a[1], b[0]))


def cost(products, megabytes):
    flops = int(products * 3 * 2 * HALF * W * 2 * W)
    return pl.CostEstimate(flops=flops, bytes_accessed=megabytes << 20, transcendentals=0)


def live(ref, kind, index):
    inside = (index >= 0) & (index <= LAST - kind)
    return inside & (ref[kind, jnp.clip(index, 0, LAST)] == 1)


def moved(value, axis, target):
    count = lax.axis_size(axis)
    pairs = [(i, target(i)) for i in range(count)]
    return lax.ppermute(value, axis, [(i, j) for i, j in pairs if 0 <= j < count])


def moved_on(value, pairs):
    return lax.ppermute(
        value, ("row", "col"), [(r * GRID_COLS + c, t * GRID_COLS + d) for (r, c), (t, d) in pairs]
    )


def everywhere(test, target):
    return [((r, c), target(r, c)) for r in range(GRID_ROWS) for c in range(GRID_COLS) if test(r, c)]


def swapped(value, pairs):
    return moved_on(value, pairs + [(b, a) for a, b in pairs])


def in_order(pieces, x, y):
    return slice((y * RING + x) * 32, (y * RING + x) * 32 + 32), split(pieces[x, y])


def borders_kernel(pieces, fb_high, fb_low):
    for x in range(RING):
        for y in range(RING):
            rows, (high, low) = in_order(pieces, x, y)
            for side in range(2):
                lanes = slice(side * HALF, side * HALF + HALF)
                fb_high[side, rows, :] = high[:, lanes]
                fb_low[side, rows, :] = low[:, lanes]


def left_kernel(where, lives, pieces, h0, h1, send_a, send_b, d_high, d_low):
    row, col = where[0], where[1]
    for x in range(RING):
        for y in range(RING):
            rows, (high, low) = in_order(pieces, x, y)
            d_high[rows, :] = high
            d_low[rows, :] = low
    odd = lax.rem(row, 2) == 1
    live_row = live(lives, 0, row)
    factor = (d_high[...], d_low[...])
    for s, h in enumerate((h0, h1)):
        lanes = slice(s * W, s * W + W)
        value = h[...]
        turned = product(factor, split(value), ((0,), (0,)))
        value = jnp.where((col + GRID_COLS * s >= row) & live_row, turned, value)
        send_a[:, lanes] = jnp.where(odd, value[:HALF], value[HALF:])
        send_b[:, lanes] = jnp.where(odd, value[HALF:], value[:HALF])


def prepare_kernel(where, gathered, high, low):
    for index in range(16):
        rows = slice(32 * index, 32 * index + 32)
        high[0, rows, :], low[0, rows, :] = split(gathered[lax.rem(where[1] + index, 16), 0])


def middle_kernel(first, where, lives, own, got, fb_high, fb_low, c_high, c_low, kept, side, edge0, edge1):
    row, col = where[0], where[1]
    odd = lax.rem(row, 2) == 1
    top = odd if first else ~odd
    top_index = top.astype(jnp.int32)
    active = live(lives, 1, jnp.where(top, row - 1, row))
    factor = (fb_high[top_index], fb_low[top_index])
    below_part = (fb_high[top_index, HALF:, :], fb_low[top_index, HALF:, :])
    odd_col = lax.rem(col, 2) == 1
    is_corner = (lax.broadcasted_iota(jnp.int32, (HALF, 128), 0) == 0) & (
        lax.broadcasted_iota(jnp.int32, (HALF, 128), 1) == 127
    )
    ends = []
    for s in range(2):
        lanes = slice(s * W, s * W + W)
        tile = col + GRID_COLS * s
        own_raw, got_raw = own[:, lanes], got[:, lanes]
        own_value = jnp.where(top & (tile < row), 0.0, own_raw)
        got_value = jnp.where(top | (tile > row), got_raw, 0.0)
        acted = active & (tile >= jnp.where(top, row - 1, row))
        upper, lower = jnp.where(top, got_value, own_value), jnp.where(top, own_value, got_value)
        rows = product(factor, split(jnp.concatenate([upper, lower], 0)), ((0,), (0,)))
        value = jnp.where(acted, rows, own_value)
        for_left = jnp.where(top, jnp.where(tile >= row, value, 0.0), jnp.where(tile == row, own_value, value))
        turns = live(lives, 0, tile)
        matrix = lambda a, b: (c_high[s, :, a:b], c_low[s, :, a:b])
        left = product(split(for_left), matrix(0, HALF), ((1,), (0,)))
        right = product(split(value), matrix(HALF, W), ((1,), (0,)))
        left = jnp.where(turns, left, for_left[:, :HALF])
        right = jnp.where(turns, right, value[:, HALF:])
        kept[2 * s] = left
        kept[2 * s + 1] = right
        has_corner = (top & (tile == row - 1)) | (~top & (tile == row) & acted)
        corner = jnp.where(has_corner & is_corner, jnp.where(top, own_raw[:, W - 128 :], got_raw[:, W - 128 :]), 0.0)
        spread = jnp.where(acted, product(below_part, split(corner), ((0,), (0,))), corner)
        kept[2 * s + 1, :, HALF - 128 :] = kept[2 * s + 1, :, HALF - 128 :] + spread
        right = kept[2 * s + 1]
        side[s] = jnp.where(odd_col, left, right)
        ends.append((left, right))
    crosses = col == 0
    edge0[...] = jnp.where(odd_col, ends[0][1], jnp.where(crosses, ends[1][0], ends[0][0]))
    edge1[...] = jnp.where(odd_col, ends[1][1], ends[1][0])


def last_kernel(first, where, lives, kept, side, edge1, edge0, c_high, c_low, *rest):
    out = rest[-1]
    row, col = where[0], where[1]
    odd = lax.rem(row, 2) == 1
    top = odd if first else ~odd
    odd_col = lax.rem(col, 2) == 1
    for s in range(2):
        tile = col + GRID_COLS * s
        left, right = kept[2 * s], kept[2 * s + 1]
        near = side[s]
        far = (edge0 if s == 0 else edge1)[...]
        if s == 1:
            far = jnp.where(col == 0, edge0[...], far)
        pairs = (
            (jnp.where(odd_col, near, far), left, W + HALF, live(lives, 1, tile - 1) & ((row < tile) | ((row == tile) & top))),
            (right, jnp.where(odd_col, far, near), W, live(lives, 1, tile) & ((row <= tile) | ((row == tile + 1) & top))),
        )
        for index, (one, two, at, keep) in enumerate(pairs):
            factor = (c_high[s, :, at : at + HALF], c_low[s, :, at : at + HALF])
            value = product(split(jnp.concatenate([one, two], 1)), factor, ((1,), (0,)))
            value = jnp.where(keep, value, two if index == 0 else one)
            out[:, s, index * HALF : index * HALF + HALF] = value


def shards(hessenberg, diag_factors, border_factors, window_live):
    row = lax.axis_index("row")
    col = lax.axis_index("col")
    where = jnp.stack([row, col]).astype(jnp.int32)
    shape = jax.ShapeDtypeStruct

    border = border_factors[0]
    above = moved(border[:, HALF:], "row", lambda r: r + 1)
    piece = jnp.concatenate([diag_factors[0], border[:, :HALF], above], 1)

    mine = moved_on(piece, everywhere(lambda r, c: True, lambda r, c: (r // 16 * 16 + (r + c) % 16, r % 16)))
    other = moved(mine, "row", lambda r: r ^ 16)
    groups = [list(range(16)), list(range(16, 32))]
    gathered = lax.all_gather(jnp.concatenate([mine, other], 0), "row", axis=0, tiled=True, axis_index_groups=groups)
    gathered = gathered.reshape(16, 2, 32, 2 * W)

    def shared(value, groups):
        every = jnp.broadcast_to(value[None], (RING, *value.shape))
        return lax.all_to_all(every, "col", 0, 0, axis_index_groups=groups)

    by_y = shared(piece, [[x + RING * y for y in range(RING)] for x in range(RING)])
    by_y = by_y.reshape(RING * 32, 2 * W)
    along_x = [[x + RING * y for x in range(RING)] for y in range(RING)]
    diag_row = shared(by_y[:, :W], along_x).reshape(RING, RING, 32, W)
    border_y, gathered = lax.optimization_barrier((by_y[:, W:], gathered))
    border_row = shared(border_y, along_x).reshape(RING, RING, 32, W)
    fb_high, fb_low = pl.pallas_call(
        borders_kernel,
        out_shape=[shape((2, W, HALF), BF16)] * 2,
        in_specs=[VMEM],
        out_specs=[VMEM] * 2,
        compiler_params=PARAMS,
        cost_estimate=cost(0, 2),
        name="borders",
    )(border_row)

    send_a, send_b = pl.pallas_call(
        left_kernel,
        out_shape=[shape((HALF, 2 * W), F32)] * 2,
        in_specs=[SMEM, SMEM] + [VMEM] * 3,
        out_specs=[VMEM] * 2,
        scratch_shapes=[pltpu.VMEM((W, W), BF16)] * 2,
        compiler_params=PARAMS,
        cost_estimate=cost(2, 7),
        name="left",
    )(where, window_live, diag_row, hessenberg[:, 0], hessenberg[:, 1])

    every_col = range(GRID_COLS)
    got_b = swapped(send_b, [((r, c), (r + 1, c)) for r in range(1, 31, 2) for c in every_col])
    got_a = swapped(send_a, [((r, c), (r + 1, c)) for r in range(0, 32, 2) for c in every_col])

    c_high, c_low = pl.pallas_call(
        prepare_kernel,
        out_shape=[shape((2, W, 2 * W), BF16)] * 2,
        grid_spec=pltpu.PrefetchScalarGridSpec(
            num_scalar_prefetch=1,
            grid=(2,),
            in_specs=[pl.BlockSpec((16, 1, 32, 2 * W), lambda s, where: (0, s ^ (where[0] // 16), 0, 0))],
            out_specs=[pl.BlockSpec((1, W, 2 * W), lambda s, where: (s, 0, 0))] * 2,
        ),
        compiler_params=PARAMS,
        cost_estimate=cost(0, 8),
        name="prepare",
    )(where, gathered)

    def middle(first, own, got):
        return pl.pallas_call(
            functools.partial(middle_kernel, first),
            out_shape=[shape((4, HALF, HALF), F32), shape((2, HALF, HALF), F32)] + [shape((HALF, HALF), F32)] * 2,
            in_specs=[SMEM, SMEM] + [VMEM] * 6,
            out_specs=[VMEM] * 4,
            compiler_params=PARAMS,
            cost_estimate=cost(2, 4),
            name="middle",
        )(where, window_live, own, got, fb_high, fb_low, c_high, c_low)

    def exchanged(side, edge0, edge1):
        rows = range(GRID_ROWS)
        side = swapped(side, [((r, c), (r, c + 1)) for r in rows for c in range(0, 16, 2) if r <= c + 17])
        edge0 = swapped(edge0, [((r, c), (r, (c + 1) % 16)) for r in rows for c in range(1, 16, 2) if r <= c + 1])
        edge1 = swapped(edge1, [((r, c), (r, c + 1)) for r in rows for c in range(1, 15, 2) if r <= c + 17])
        return side, edge1, edge0

    def last(first, kept, moved_parts, *done):
        place = lambda i, where: (lax.rem(where[0], 2) ^ (1 if first else 0), 0, 0)
        whole = lambda shape: pl.BlockSpec(shape, lambda i, where: (0,) * len(shape))
        lives = pl.BlockSpec(memory_space=pltpu.SMEM)
        specs = [
            lives,
            whole((4, HALF, HALF)),
            whole((2, HALF, HALF)),
            whole((HALF, HALF)),
            whole((HALF, HALF)),
            whole((2, W, 2 * W)),
            whole((2, W, 2 * W)),
        ]
        return pl.pallas_call(
            functools.partial(last_kernel, first),
            out_shape=shape((W, 2, W), F32),
            grid_spec=pltpu.PrefetchScalarGridSpec(
                num_scalar_prefetch=1,
                grid=(1,),
                in_specs=specs + [pl.BlockSpec(memory_space=pl.ANY)] * len(done),
                out_specs=pl.BlockSpec((HALF, 2, W), place),
            ),
            input_output_aliases={8: 0} if done else {},
            compiler_params=PARAMS,
            cost_estimate=cost(1, 4),
            name="last",
        )(where, window_live, kept, *moved_parts, c_high, c_low, *done)

    kept_a, *ends_a = middle(True, send_a, got_a)
    parts_a = exchanged(*ends_a)
    kept_b, *ends_b = middle(False, send_b, got_b)
    parts_b = exchanged(*ends_b)
    out = last(True, kept_a, parts_a)
    return last(False, kept_b, parts_b, out)


def solution(mesh):
    in_specs = (P("row", None, "col"), P("row", "col", None), P("row", "col", None), P())
    out_specs = P("row", None, "col")
    return jax.shard_map(shards, mesh=mesh, in_specs=in_specs, out_specs=out_specs, check_vma=False)
```

```python
import functools

import jax
import jax.numpy as jnp
from jax import lax
from jax.experimental import pallas as pl
from jax.experimental.pallas import tpu as pltpu
from jax.sharding import PartitionSpec as P

GRID_ROWS, GRID_COLS = 32, 16
RING = 4
W = 512
HALF = 256
LAST = 31
BF16, F32 = jnp.bfloat16, jnp.float32
PARAMS = pltpu.CompilerParams(vmem_limit_bytes=16 * 1024 * 1024)
VMEM = pl.BlockSpec(memory_space=pltpu.VMEM)
SMEM = pl.BlockSpec(memory_space=pltpu.SMEM)


def split(x):
    high = x.astype(BF16)
    return high, (x - high.astype(F32)).astype(BF16)


def product(a, b, contract):
    dims = (contract, ((), ()))
    one = lambda x, y: lax.dot_general(x, y, dims, preferred_element_type=F32)
    return one(a[0], b[0]) + (one(a[0], b[1]) + one(a[1], b[0]))


def cost(products, megabytes):
    flops = int(products * 3 * 2 * HALF * W * 2 * W)
    return pl.CostEstimate(flops=flops, bytes_accessed=megabytes << 20, transcendentals=0)


def live(ref, kind, index):
    inside = (index >= 0) & (index <= LAST - kind)
    return inside & (ref[kind, jnp.clip(index, 0, LAST)] == 1)


def moved(value, axis, target):
    count = lax.axis_size(axis)
    pairs = [(i, target(i)) for i in range(count)]
    return lax.ppermute(value, axis, [(i, j) for i, j in pairs if 0 <= j < count])


def moved_on(value, pairs):
    return lax.ppermute(
        value, ("row", "col"), [(r * GRID_COLS + c, t * GRID_COLS + d) for (r, c), (t, d) in pairs]
    )


def everywhere(test, target):
    return [((r, c), target(r, c)) for r in range(GRID_ROWS) for c in range(GRID_COLS) if test(r, c)]


def swapped(value, pairs):
    return moved_on(value, pairs + [(b, a) for a, b in pairs])


def left_kernel(where, lives, pieces, h0, h1, send_a, send_b0, send_b1, fb_high, fb_low, d_high, d_low):
    row, col = where[0], where[1]
    for x in range(RING):
        for y in range(RING):
            rows = slice((y * RING + x) * 32, (y * RING + x) * 32 + 32)
            high, low = split(pieces[x, y])
            for side in range(2):
                lanes = slice(W + side * HALF, W + side * HALF + HALF)
                fb_high[side, rows, :] = high[:, lanes]
                fb_low[side, rows, :] = low[:, lanes]
            d_high[rows, :] = high[:, :W]
            d_low[rows, :] = low[:, :W]
    odd = lax.rem(row, 2) == 1
    live_row = live(lives, 0, row)
    factor = (d_high[...], d_low[...])
    for s, h in enumerate((h0, h1)):
        lanes = slice(s * W, s * W + W)
        value = h[...]
        turned = product(factor, split(value), ((0,), (0,)))
        value = jnp.where((col + GRID_COLS * s >= row) & live_row, turned, value)
        send_a[:, lanes] = jnp.where(odd, value[:HALF], value[HALF:])
        (send_b0, send_b1)[s][...] = jnp.where(odd, value[HALF:], value[:HALF])


def prepare_kernel(where, gathered, high, low):
    for index in range(16):
        rows = slice(32 * index, 32 * index + 32)
        high[0, rows, :], low[0, rows, :] = split(gathered[lax.rem(where[1] + index, 16), 0])


def middle_kernel(first, where, lives, own0, own1, got0, got1, fb_high, fb_low, c_high, c_low, kept, side, edge0, edge1):
    row, col = where[0], where[1]
    odd = lax.rem(row, 2) == 1
    top = odd if first else ~odd
    top_index = top.astype(jnp.int32)
    active = live(lives, 1, jnp.where(top, row - 1, row))
    factor = (fb_high[top_index], fb_low[top_index])
    below_part = (fb_high[top_index, HALF:, :], fb_low[top_index, HALF:, :])
    odd_col = lax.rem(col, 2) == 1
    is_corner = (lax.broadcasted_iota(jnp.int32, (HALF, 128), 0) == 0) & (
        lax.broadcasted_iota(jnp.int32, (HALF, 128), 1) == 127
    )
    part = lambda ref, lanes: ref[:, lanes] if first else ref[...]
    ends = []
    for s in range(2):
        lanes = slice(s * W, s * W + W)
        tile = col + GRID_COLS * s
        own_raw, got_raw = (part((own0, own1)[s], lanes), part((got0, got1)[s], lanes))
        own_value = jnp.where(top & (tile < row), 0.0, own_raw)
        got_value = jnp.where(top | (tile > row), got_raw, 0.0)
        acted = active & (tile >= jnp.where(top, row - 1, row))
        upper, lower = jnp.where(top, got_value, own_value), jnp.where(top, own_value, got_value)
        rows = product(factor, split(jnp.concatenate([upper, lower], 0)), ((0,), (0,)))
        value = jnp.where(acted, rows, own_value)
        for_left = jnp.where(top, jnp.where(tile >= row, value, 0.0), jnp.where(tile == row, own_value, value))
        turns = live(lives, 0, tile)
        matrix = lambda a, b: (c_high[s, :, a:b], c_low[s, :, a:b])
        left = product(split(for_left), matrix(0, HALF), ((1,), (0,)))
        right = product(split(value), matrix(HALF, W), ((1,), (0,)))
        left = jnp.where(turns, left, for_left[:, :HALF])
        right = jnp.where(turns, right, value[:, HALF:])
        kept[2 * s] = left
        kept[2 * s + 1] = right
        has_corner = (top & (tile == row - 1)) | (~top & (tile == row) & acted)
        corner = jnp.where(has_corner & is_corner, jnp.where(top, own_raw[:, W - 128 :], got_raw[:, W - 128 :]), 0.0)
        spread = jnp.where(acted, product(below_part, split(corner), ((0,), (0,))), corner)
        kept[2 * s + 1, :, HALF - 128 :] = kept[2 * s + 1, :, HALF - 128 :] + spread
        right = kept[2 * s + 1]
        side[s] = jnp.where(odd_col, left, right)
        ends.append((left, right))
    crosses = col == 0
    edge0[...] = jnp.where(odd_col, ends[0][1], jnp.where(crosses, ends[1][0], ends[0][0]))
    edge1[...] = jnp.where(odd_col, ends[1][1], ends[1][0])


def last_kernel(first, where, lives, kept, side, edge1, edge0, c_high, c_low, *rest):
    out = rest[-1]
    row, col = where[0], where[1]
    odd = lax.rem(row, 2) == 1
    top = odd if first else ~odd
    odd_col = lax.rem(col, 2) == 1
    for s in range(2):
        tile = col + GRID_COLS * s
        left, right = kept[2 * s], kept[2 * s + 1]
        near = side[s]
        far = (edge0 if s == 0 else edge1)[...]
        if s == 1:
            far = jnp.where(col == 0, edge0[...], far)
        pairs = (
            (jnp.where(odd_col, near, far), left, W + HALF, live(lives, 1, tile - 1) & ((row < tile) | ((row == tile) & top))),
            (right, jnp.where(odd_col, far, near), W, live(lives, 1, tile) & ((row <= tile) | ((row == tile + 1) & top))),
        )
        for index, (one, two, at, keep) in enumerate(pairs):
            factor = (c_high[s, :, at : at + HALF], c_low[s, :, at : at + HALF])
            value = product(split(jnp.concatenate([one, two], 1)), factor, ((1,), (0,)))
            value = jnp.where(keep, value, two if index == 0 else one)
            out[:, s, index * HALF : index * HALF + HALF] = value


def shards(hessenberg, diag_factors, border_factors, window_live):
    row = lax.axis_index("row")
    col = lax.axis_index("col")
    where = jnp.stack([row, col]).astype(jnp.int32)
    shape = jax.ShapeDtypeStruct

    border = border_factors[0]
    above = moved(border[:, HALF:], "row", lambda r: r + 1)
    piece = jnp.concatenate([diag_factors[0], border[:, :HALF], above], 1)

    mine = moved_on(piece, everywhere(lambda r, c: True, lambda r, c: (r // 16 * 16 + (r + c) % 16, r % 16)))
    other = moved(mine, "row", lambda r: r ^ 16)
    groups = [list(range(16)), list(range(16, 32))]
    gathered = lax.all_gather(jnp.concatenate([mine, other], 0), "row", axis=0, tiled=True, axis_index_groups=groups)
    gathered = gathered.reshape(16, 2, 32, 2 * W)

    def shared(value, groups):
        every = jnp.broadcast_to(value[None], (RING, *value.shape))
        return lax.all_to_all(every, "col", 0, 0, axis_index_groups=groups)

    by_y = shared(piece, [[x + RING * y for y in range(RING)] for x in range(RING)])
    along_x = [[x + RING * y for x in range(RING)] for y in range(RING)]
    by_row = shared(by_y.reshape(RING * 32, 2 * W), along_x).reshape(RING, RING, 32, 2 * W)

    send_a, send_b0, send_b1, fb_high, fb_low = pl.pallas_call(
        left_kernel,
        out_shape=[shape((HALF, 2 * W), F32)] + [shape((HALF, W), F32)] * 2 + [shape((2, W, HALF), BF16)] * 2,
        in_specs=[SMEM, SMEM] + [VMEM] * 3,
        out_specs=[VMEM] * 5,
        scratch_shapes=[pltpu.VMEM((W, W), BF16)] * 2,
        compiler_params=PARAMS,
        cost_estimate=cost(2, 7),
        name="left",
    )(where, window_live, by_row, hessenberg[:, 0], hessenberg[:, 1])

    every_col = range(GRID_COLS)
    pairs = [((r, c), (r + 1, c)) for r in range(1, 31, 2) for c in every_col]
    got_b1 = swapped(send_b1, [(a, b) for a, b in pairs if a[1] + GRID_COLS >= a[0]])
    got_b0 = swapped(send_b0, [(a, b) for a, b in pairs if a[1] >= a[0]])
    got_a = swapped(send_a, [((r, c), (r + 1, c)) for r in range(0, 32, 2) for c in every_col])

    c_high, c_low = pl.pallas_call(
        prepare_kernel,
        out_shape=[shape((2, W, 2 * W), BF16)] * 2,
        grid_spec=pltpu.PrefetchScalarGridSpec(
            num_scalar_prefetch=1,
            grid=(2,),
            in_specs=[pl.BlockSpec((16, 1, 32, 2 * W), lambda s, where: (0, s ^ (where[0] // 16), 0, 0))],
            out_specs=[pl.BlockSpec((1, W, 2 * W), lambda s, where: (s, 0, 0))] * 2,
        ),
        compiler_params=PARAMS,
        cost_estimate=cost(0, 8),
        name="prepare",
    )(where, gathered)

    def middle(first, *parts):
        return pl.pallas_call(
            functools.partial(middle_kernel, first),
            out_shape=[shape((4, HALF, HALF), F32), shape((2, HALF, HALF), F32)] + [shape((HALF, HALF), F32)] * 2,
            in_specs=[SMEM, SMEM] + [VMEM] * 8,
            out_specs=[VMEM] * 4,
            compiler_params=PARAMS,
            cost_estimate=cost(2, 4),
            name="middle",
        )(where, window_live, *parts, fb_high, fb_low, c_high, c_low)

    def exchanged(side, edge0, edge1):
        rows = range(GRID_ROWS)
        side = swapped(side, [((r, c), (r, c + 1)) for r in rows for c in range(0, 16, 2) if r <= c + 17])
        edge0 = swapped(edge0, [((r, c), (r, (c + 1) % 16)) for r in rows for c in range(1, 16, 2) if r <= c + 1])
        edge1 = swapped(edge1, [((r, c), (r, c + 1)) for r in rows for c in range(1, 15, 2) if r <= c + 17])
        return side, edge1, edge0

    def last(first, kept, moved_parts, *done):
        place = lambda i, where: (lax.rem(where[0], 2) ^ (1 if first else 0), 0, 0)
        whole = lambda shape: pl.BlockSpec(shape, lambda i, where: (0,) * len(shape))
        lives = pl.BlockSpec(memory_space=pltpu.SMEM)
        specs = [
            lives,
            whole((4, HALF, HALF)),
            whole((2, HALF, HALF)),
            whole((HALF, HALF)),
            whole((HALF, HALF)),
            whole((2, W, 2 * W)),
            whole((2, W, 2 * W)),
        ]
        return pl.pallas_call(
            functools.partial(last_kernel, first),
            out_shape=shape((W, 2, W), F32),
            grid_spec=pltpu.PrefetchScalarGridSpec(
                num_scalar_prefetch=1,
                grid=(1,),
                in_specs=specs + [pl.BlockSpec(memory_space=pl.ANY)] * len(done),
                out_specs=pl.BlockSpec((HALF, 2, W), place),
            ),
            input_output_aliases={8: 0} if done else {},
            compiler_params=PARAMS,
            cost_estimate=cost(1, 4),
            name="last",
        )(where, window_live, kept, *moved_parts, c_high, c_low, *done)

    kept_a, *ends_a = middle(True, send_a, send_a, got_a, got_a)
    parts_a = exchanged(*ends_a)
    kept_b, *ends_b = middle(False, send_b0, send_b1, got_b0, got_b1)
    parts_b = exchanged(*ends_b)
    out = last(True, kept_a, parts_a)
    return last(False, kept_b, parts_b, out)


def solution(mesh):
    in_specs = (P("row", None, "col"), P("row", "col", None), P("row", "col", None), P())
    out_specs = P("row", None, "col")
    return jax.shard_map(shards, mesh=mesh, in_specs=in_specs, out_specs=out_specs, check_vma=False)
```

```python
import functools

import jax
import jax.numpy as jnp
from jax import lax
from jax.experimental import pallas as pl
from jax.experimental.pallas import tpu as pltpu
from jax.sharding import PartitionSpec as P

GRID_ROWS, GRID_COLS = 32, 16
RING = 4
W = 512
HALF = 256
LAST = 31
BF16, F32 = jnp.bfloat16, jnp.float32
PARAMS = pltpu.CompilerParams(vmem_limit_bytes=16 * 1024 * 1024)
VMEM = pl.BlockSpec(memory_space=pltpu.VMEM)
SMEM = pl.BlockSpec(memory_space=pltpu.SMEM)


def split(x):
    high = x.astype(BF16)
    return high, (x - high.astype(F32)).astype(BF16)


def product(a, b, contract):
    dims = (contract, ((), ()))
    one = lambda x, y: lax.dot_general(x, y, dims, preferred_element_type=F32)
    return one(a[0], b[0]) + (one(a[0], b[1]) + one(a[1], b[0]))


def cost(products, megabytes):
    flops = int(products * 3 * 2 * HALF * W * 2 * W)
    return pl.CostEstimate(flops=flops, bytes_accessed=megabytes << 20, transcendentals=0)


def live(ref, kind, index):
    inside = (index >= 0) & (index <= LAST - kind)
    return inside & (ref[kind, jnp.clip(index, 0, LAST)] == 1)


def moved(value, axis, target):
    count = lax.axis_size(axis)
    pairs = [(i, target(i)) for i in range(count)]
    return lax.ppermute(value, axis, [(i, j) for i, j in pairs if 0 <= j < count])


def moved_on(value, pairs):
    return lax.ppermute(
        value, ("row", "col"), [(r * GRID_COLS + c, t * GRID_COLS + d) for (r, c), (t, d) in pairs]
    )


def everywhere(test, target):
    return [((r, c), target(r, c)) for r in range(GRID_ROWS) for c in range(GRID_COLS) if test(r, c)]


def swapped(value, pairs):
    return moved_on(value, pairs + [(b, a) for a, b in pairs])


def borders_kernel(pieces, fb_high, fb_low):
    for x in range(RING):
        for y in range(RING):
            rows = slice((y * RING + x) * 32, (y * RING + x) * 32 + 32)
            high, low = split(pieces[x, y, :, W:])
            for side in range(2):
                lanes = slice(side * HALF, side * HALF + HALF)
                fb_high[side, rows, :] = high[:, lanes]
                fb_low[side, rows, :] = low[:, lanes]


def left_kernel(where, lives, pieces, h0, h1, send_a, send_b0, send_b1, d_high, d_low):
    row, col = where[0], where[1]
    for x in range(RING):
        for y in range(RING):
            rows = slice((y * RING + x) * 32, (y * RING + x) * 32 + 32)
            high, low = split(pieces[x, y, :, :W])
            d_high[rows, :] = high
            d_low[rows, :] = low
    odd = lax.rem(row, 2) == 1
    live_row = live(lives, 0, row)
    factor = (d_high[...], d_low[...])
    for s, h in enumerate((h0, h1)):
        lanes = slice(s * W, s * W + W)
        value = h[...]
        turned = product(factor, split(value), ((0,), (0,)))
        value = jnp.where((col + GRID_COLS * s >= row) & live_row, turned, value)
        send_a[:, lanes] = jnp.where(odd, value[:HALF], value[HALF:])
        (send_b0, send_b1)[s][...] = jnp.where(odd, value[HALF:], value[:HALF])


def prepare_kernel(where, gathered, high, low):
    for index in range(16):
        rows = slice(32 * index, 32 * index + 32)
        high[0, rows, :], low[0, rows, :] = split(gathered[lax.rem(where[1] + index, 16), 0])


def middle_kernel(first, where, lives, own0, own1, got0, got1, fb_high, fb_low, c_high, c_low, kept, side, edge0, edge1):
    row, col = where[0], where[1]
    odd = lax.rem(row, 2) == 1
    top = odd if first else ~odd
    top_index = top.astype(jnp.int32)
    active = live(lives, 1, jnp.where(top, row - 1, row))
    factor = (fb_high[top_index], fb_low[top_index])
    below_part = (fb_high[top_index, HALF:, :], fb_low[top_index, HALF:, :])
    odd_col = lax.rem(col, 2) == 1
    is_corner = (lax.broadcasted_iota(jnp.int32, (HALF, 128), 0) == 0) & (
        lax.broadcasted_iota(jnp.int32, (HALF, 128), 1) == 127
    )
    part = lambda ref, lanes: ref[:, lanes] if first else ref[...]
    ends = []
    for s in range(2):
        lanes = slice(s * W, s * W + W)
        tile = col + GRID_COLS * s
        own_raw, got_raw = (part((own0, own1)[s], lanes), part((got0, got1)[s], lanes))
        own_value = jnp.where(top & (tile < row), 0.0, own_raw)
        got_value = jnp.where(top | (tile > row), got_raw, 0.0)
        acted = active & (tile >= jnp.where(top, row - 1, row))
        upper, lower = jnp.where(top, got_value, own_value), jnp.where(top, own_value, got_value)
        rows = product(factor, split(jnp.concatenate([upper, lower], 0)), ((0,), (0,)))
        value = jnp.where(acted, rows, own_value)
        for_left = jnp.where(top, jnp.where(tile >= row, value, 0.0), jnp.where(tile == row, own_value, value))
        turns = live(lives, 0, tile)
        matrix = lambda a, b: (c_high[s, :, a:b], c_low[s, :, a:b])
        left = product(split(for_left), matrix(0, HALF), ((1,), (0,)))
        right = product(split(value), matrix(HALF, W), ((1,), (0,)))
        left = jnp.where(turns, left, for_left[:, :HALF])
        right = jnp.where(turns, right, value[:, HALF:])
        kept[2 * s] = left
        kept[2 * s + 1] = right
        has_corner = (top & (tile == row - 1)) | (~top & (tile == row) & acted)
        corner = jnp.where(has_corner & is_corner, jnp.where(top, own_raw[:, W - 128 :], got_raw[:, W - 128 :]), 0.0)
        spread = jnp.where(acted, product(below_part, split(corner), ((0,), (0,))), corner)
        kept[2 * s + 1, :, HALF - 128 :] = kept[2 * s + 1, :, HALF - 128 :] + spread
        right = kept[2 * s + 1]
        side[s] = jnp.where(odd_col, left, right)
        ends.append((left, right))
    crosses = col == 0
    edge0[...] = jnp.where(odd_col, ends[0][1], jnp.where(crosses, ends[1][0], ends[0][0]))
    edge1[...] = jnp.where(odd_col, ends[1][1], ends[1][0])


def last_kernel(first, where, lives, kept, side, edge1, edge0, c_high, c_low, *rest):
    out = rest[-1]
    row, col = where[0], where[1]
    odd = lax.rem(row, 2) == 1
    top = odd if first else ~odd
    odd_col = lax.rem(col, 2) == 1
    for s in range(2):
        tile = col + GRID_COLS * s
        left, right = kept[2 * s], kept[2 * s + 1]
        near = side[s]
        far = (edge0 if s == 0 else edge1)[...]
        if s == 1:
            far = jnp.where(col == 0, edge0[...], far)
        pairs = (
            (jnp.where(odd_col, near, far), left, W + HALF, live(lives, 1, tile - 1) & ((row < tile) | ((row == tile) & top))),
            (right, jnp.where(odd_col, far, near), W, live(lives, 1, tile) & ((row <= tile) | ((row == tile + 1) & top))),
        )
        for index, (one, two, at, keep) in enumerate(pairs):
            factor = (c_high[s, :, at : at + HALF], c_low[s, :, at : at + HALF])
            value = product(split(jnp.concatenate([one, two], 1)), factor, ((1,), (0,)))
            value = jnp.where(keep, value, two if index == 0 else one)
            out[:, s, index * HALF : index * HALF + HALF] = value


def shards(hessenberg, diag_factors, border_factors, window_live):
    row = lax.axis_index("row")
    col = lax.axis_index("col")
    where = jnp.stack([row, col]).astype(jnp.int32)
    shape = jax.ShapeDtypeStruct

    border = border_factors[0]
    above = moved(border[:, HALF:], "row", lambda r: r + 1)
    piece = jnp.concatenate([diag_factors[0], border[:, :HALF], above], 1)

    mine = moved_on(piece, everywhere(lambda r, c: True, lambda r, c: (r // 16 * 16 + (r + c) % 16, r % 16)))
    other = moved(mine, "row", lambda r: r ^ 16)
    groups = [list(range(16)), list(range(16, 32))]
    gathered = lax.all_gather(jnp.concatenate([mine, other], 0), "row", axis=0, tiled=True, axis_index_groups=groups)
    gathered = gathered.reshape(16, 2, 32, 2 * W)

    def shared(value, groups):
        every = jnp.broadcast_to(value[None], (RING, *value.shape))
        return lax.all_to_all(every, "col", 0, 0, axis_index_groups=groups)

    by_y = shared(piece, [[x + RING * y for y in range(RING)] for x in range(RING)])
    along_x = [[x + RING * y for x in range(RING)] for y in range(RING)]
    by_row = shared(by_y.reshape(RING * 32, 2 * W), along_x).reshape(RING, RING, 32, 2 * W)

    send_a, send_b0, send_b1 = pl.pallas_call(
        left_kernel,
        out_shape=[shape((HALF, 2 * W), F32)] + [shape((HALF, W), F32)] * 2,
        in_specs=[SMEM, SMEM] + [VMEM] * 3,
        out_specs=[VMEM] * 3,
        scratch_shapes=[pltpu.VMEM((W, W), BF16)] * 2,
        compiler_params=PARAMS,
        cost_estimate=cost(2, 7),
        name="left",
    )(where, window_live, by_row, hessenberg[:, 0], hessenberg[:, 1])
    fb_high, fb_low = pl.pallas_call(
        borders_kernel,
        out_shape=[shape((2, W, HALF), BF16)] * 2,
        in_specs=[VMEM],
        out_specs=[VMEM] * 2,
        compiler_params=PARAMS,
        cost_estimate=cost(0, 2),
        name="borders",
    )(by_row)

    every_col = range(GRID_COLS)
    pairs = [((r, c), (r + 1, c)) for r in range(1, 31, 2) for c in every_col]
    got_b1 = swapped(send_b1, [(a, b) for a, b in pairs if a[1] + GRID_COLS >= a[0]])
    got_b0 = swapped(send_b0, [(a, b) for a, b in pairs if a[1] >= a[0]])
    got_a = swapped(send_a, [((r, c), (r + 1, c)) for r in range(0, 32, 2) for c in every_col])

    c_high, c_low = pl.pallas_call(
        prepare_kernel,
        out_shape=[shape((2, W, 2 * W), BF16)] * 2,
        grid_spec=pltpu.PrefetchScalarGridSpec(
            num_scalar_prefetch=1,
            grid=(2,),
            in_specs=[pl.BlockSpec((16, 1, 32, 2 * W), lambda s, where: (0, s ^ (where[0] // 16), 0, 0))],
            out_specs=[pl.BlockSpec((1, W, 2 * W), lambda s, where: (s, 0, 0))] * 2,
        ),
        compiler_params=PARAMS,
        cost_estimate=cost(0, 8),
        name="prepare",
    )(where, gathered)

    def middle(first, *parts):
        return pl.pallas_call(
            functools.partial(middle_kernel, first),
            out_shape=[shape((4, HALF, HALF), F32), shape((2, HALF, HALF), F32)] + [shape((HALF, HALF), F32)] * 2,
            in_specs=[SMEM, SMEM] + [VMEM] * 8,
            out_specs=[VMEM] * 4,
            compiler_params=PARAMS,
            cost_estimate=cost(2, 4),
            name="middle",
        )(where, window_live, *parts, fb_high, fb_low, c_high, c_low)

    def exchanged(side, edge0, edge1):
        rows = range(GRID_ROWS)
        side = swapped(side, [((r, c), (r, c + 1)) for r in rows for c in range(0, 16, 2) if r <= c + 17])
        edge0 = swapped(edge0, [((r, c), (r, (c + 1) % 16)) for r in rows for c in range(1, 16, 2) if r <= c + 1])
        edge1 = swapped(edge1, [((r, c), (r, c + 1)) for r in rows for c in range(1, 15, 2) if r <= c + 17])
        return side, edge1, edge0

    def last(first, kept, moved_parts, *done):
        place = lambda i, where: (lax.rem(where[0], 2) ^ (1 if first else 0), 0, 0)
        whole = lambda shape: pl.BlockSpec(shape, lambda i, where: (0,) * len(shape))
        lives = pl.BlockSpec(memory_space=pltpu.SMEM)
        specs = [
            lives,
            whole((4, HALF, HALF)),
            whole((2, HALF, HALF)),
            whole((HALF, HALF)),
            whole((HALF, HALF)),
            whole((2, W, 2 * W)),
            whole((2, W, 2 * W)),
        ]
        return pl.pallas_call(
            functools.partial(last_kernel, first),
            out_shape=shape((W, 2, W), F32),
            grid_spec=pltpu.PrefetchScalarGridSpec(
                num_scalar_prefetch=1,
                grid=(1,),
                in_specs=specs + [pl.BlockSpec(memory_space=pl.ANY)] * len(done),
                out_specs=pl.BlockSpec((HALF, 2, W), place),
            ),
            input_output_aliases={8: 0} if done else {},
            compiler_params=PARAMS,
            cost_estimate=cost(1, 4),
            name="last",
        )(where, window_live, kept, *moved_parts, c_high, c_low, *done)

    kept_a, *ends_a = middle(True, send_a, send_a, got_a, got_a)
    parts_a = exchanged(*ends_a)
    kept_b, *ends_b = middle(False, send_b0, send_b1, got_b0, got_b1)
    parts_b = exchanged(*ends_b)
    out = last(True, kept_a, parts_a)
    return last(False, kept_b, parts_b, out)


def solution(mesh):
    in_specs = (P("row", None, "col"), P("row", "col", None), P("row", "col", None), P())
    out_specs = P("row", None, "col")
    return jax.shard_map(shards, mesh=mesh, in_specs=in_specs, out_specs=out_specs, check_vma=False)
```

```python
import functools

import jax
import jax.numpy as jnp
from jax import lax
from jax.experimental import pallas as pl
from jax.experimental.pallas import tpu as pltpu
from jax.sharding import PartitionSpec as P

GRID_ROWS, GRID_COLS = 32, 16
RING = 4
W = 512
HALF = 256
LAST = 31
BF16, F32 = jnp.bfloat16, jnp.float32
PARAMS = pltpu.CompilerParams(vmem_limit_bytes=16 * 1024 * 1024)
VMEM = pl.BlockSpec(memory_space=pltpu.VMEM)
SMEM = pl.BlockSpec(memory_space=pltpu.SMEM)


def split(x):
    high = x.astype(BF16)
    return high, (x - high.astype(F32)).astype(BF16)


def product(a, b, contract):
    dims = (contract, ((), ()))
    one = lambda x, y: lax.dot_general(x, y, dims, preferred_element_type=F32)
    return one(a[0], b[0]) + (one(a[0], b[1]) + one(a[1], b[0]))


def cost(products, megabytes):
    flops = int(products * 3 * 2 * HALF * W * 2 * W)
    return pl.CostEstimate(flops=flops, bytes_accessed=megabytes << 20, transcendentals=0)


def live(ref, kind, index):
    inside = (index >= 0) & (index <= LAST - kind)
    return inside & (ref[kind, jnp.clip(index, 0, LAST)] == 1)


def moved(value, axis, target):
    count = lax.axis_size(axis)
    pairs = [(i, target(i)) for i in range(count)]
    return lax.ppermute(value, axis, [(i, j) for i, j in pairs if 0 <= j < count])


def moved_on(value, pairs):
    return lax.ppermute(
        value, ("row", "col"), [(r * GRID_COLS + c, t * GRID_COLS + d) for (r, c), (t, d) in pairs]
    )


def everywhere(test, target):
    return [((r, c), target(r, c)) for r in range(GRID_ROWS) for c in range(GRID_COLS) if test(r, c)]


def swapped(value, pairs):
    return moved_on(value, pairs + [(b, a) for a, b in pairs])


def left_kernel(where, lives, pieces, h0, h1, send_a, send_b0, send_b1, fb_high, fb_low, d_high, d_low):
    row, col = where[0], where[1]
    for x in range(RING):
        for y in range(RING):
            rows = slice((y * RING + x) * 32, (y * RING + x) * 32 + 32)
            high, low = split(pieces[x, y])
            for side in range(2):
                lanes = slice(W + side * HALF, W + side * HALF + HALF)
                fb_high[side, rows, :] = high[:, lanes]
                fb_low[side, rows, :] = low[:, lanes]
            d_high[rows, :] = high[:, :W]
            d_low[rows, :] = low[:, :W]
    odd = lax.rem(row, 2) == 1
    live_row = live(lives, 0, row)
    factor = (d_high[...], d_low[...])
    for s, h in enumerate((h0, h1)):
        lanes = slice(s * W, s * W + W)
        value = h[...]
        turned = product(factor, split(value), ((0,), (0,)))
        value = jnp.where((col + GRID_COLS * s >= row) & live_row, turned, value)
        send_a[:, lanes] = jnp.where(odd, value[:HALF], value[HALF:])
        (send_b0, send_b1)[s][...] = jnp.where(odd, value[HALF:], value[:HALF])


def prepare_kernel(where, gathered, high, low):
    for index in range(16):
        rows = slice(32 * index, 32 * index + 32)
        high[0, rows, :], low[0, rows, :] = split(gathered[lax.rem(where[1] + index, 16), 0])


def middle_kernel(first, where, lives, own0, own1, got0, got1, fb_high, fb_low, c_high, c_low, kept, side, edge0, edge1):
    row, col = where[0], where[1]
    odd = lax.rem(row, 2) == 1
    top = odd if first else ~odd
    top_index = top.astype(jnp.int32)
    active = live(lives, 1, jnp.where(top, row - 1, row))
    factor = (fb_high[top_index], fb_low[top_index])
    below_part = (fb_high[top_index, HALF:, :], fb_low[top_index, HALF:, :])
    odd_col = lax.rem(col, 2) == 1
    is_corner = (lax.broadcasted_iota(jnp.int32, (HALF, 128), 0) == 0) & (
        lax.broadcasted_iota(jnp.int32, (HALF, 128), 1) == 127
    )
    part = lambda ref, lanes: ref[:, lanes] if first else ref[...]
    ends = []
    for s in range(2):
        lanes = slice(s * W, s * W + W)
        tile = col + GRID_COLS * s
        own_raw, got_raw = (part((own0, own1)[s], lanes), part((got0, got1)[s], lanes))
        own_value = jnp.where(top & (tile < row), 0.0, own_raw)
        got_value = jnp.where(top | (tile > row), got_raw, 0.0)
        acted = active & (tile >= jnp.where(top, row - 1, row))
        upper, lower = jnp.where(top, got_value, own_value), jnp.where(top, own_value, got_value)
        rows = product(factor, split(jnp.concatenate([upper, lower], 0)), ((0,), (0,)))
        value = jnp.where(acted, rows, own_value)
        for_left = jnp.where(top, jnp.where(tile >= row, value, 0.0), jnp.where(tile == row, own_value, value))
        turns = live(lives, 0, tile)
        matrix = lambda a, b: (c_high[s, :, a:b], c_low[s, :, a:b])
        left = product(split(for_left), matrix(0, HALF), ((1,), (0,)))
        right = product(split(value), matrix(HALF, W), ((1,), (0,)))
        left = jnp.where(turns, left, for_left[:, :HALF])
        right = jnp.where(turns, right, value[:, HALF:])
        kept[2 * s] = left
        kept[2 * s + 1] = right
        has_corner = (top & (tile == row - 1)) | (~top & (tile == row) & acted)
        corner = jnp.where(has_corner & is_corner, jnp.where(top, own_raw[:, W - 128 :], got_raw[:, W - 128 :]), 0.0)
        spread = jnp.where(acted, product(below_part, split(corner), ((0,), (0,))), corner)
        kept[2 * s + 1, :, HALF - 128 :] = kept[2 * s + 1, :, HALF - 128 :] + spread
        right = kept[2 * s + 1]
        side[s] = jnp.where(odd_col, left, right)
        ends.append((left, right))
    crosses = col == 0
    edge0[...] = jnp.where(odd_col, ends[0][1], jnp.where(crosses, ends[1][0], ends[0][0]))
    edge1[...] = jnp.where(odd_col, ends[1][1], ends[1][0])


def last_kernel(first, where, lives, kept, side, edge1, edge0, c_high, c_low, *rest):
    out = rest[-1]
    row, col = where[0], where[1]
    odd = lax.rem(row, 2) == 1
    top = odd if first else ~odd
    odd_col = lax.rem(col, 2) == 1
    for s in range(2):
        tile = col + GRID_COLS * s
        left, right = kept[2 * s], kept[2 * s + 1]
        near = side[s]
        far = (edge0 if s == 0 else edge1)[...]
        if s == 1:
            far = jnp.where(col == 0, edge0[...], far)
        pairs = (
            (jnp.where(odd_col, near, far), left, W + HALF, live(lives, 1, tile - 1) & ((row < tile) | ((row == tile) & top))),
            (right, jnp.where(odd_col, far, near), W, live(lives, 1, tile) & ((row <= tile) | ((row == tile + 1) & top))),
        )
        for index, (one, two, at, keep) in enumerate(pairs):
            factor = (c_high[s, :, at : at + HALF], c_low[s, :, at : at + HALF])
            value = product(split(jnp.concatenate([one, two], 1)), factor, ((1,), (0,)))
            value = jnp.where(keep, value, two if index == 0 else one)
            out[:, s, index * HALF : index * HALF + HALF] = value


def shards(hessenberg, diag_factors, border_factors, window_live):
    row = lax.axis_index("row")
    col = lax.axis_index("col")
    where = jnp.stack([row, col]).astype(jnp.int32)
    shape = jax.ShapeDtypeStruct

    border = border_factors[0]
    above = moved(border[:, HALF:], "row", lambda r: r + 1)
    piece = jnp.concatenate([diag_factors[0], border[:, :HALF], above], 1)

    mine = moved_on(piece, everywhere(lambda r, c: True, lambda r, c: (r // 16 * 16 + (r + c) % 16, r % 16)))
    other = moved(mine, "row", lambda r: r ^ 16)
    groups = [list(range(16)), list(range(16, 32))]
    gathered = lax.all_gather(jnp.concatenate([mine, other], 0), "row", axis=0, tiled=True, axis_index_groups=groups)
    gathered = gathered.reshape(16, 2, 32, 2 * W)

    def shared(value, groups):
        every = jnp.broadcast_to(value[None], (RING, *value.shape))
        return lax.all_to_all(every, "col", 0, 0, axis_index_groups=groups)

    by_y = shared(piece, [[x + RING * y for y in range(RING)] for x in range(RING)])
    along_x = [[x + RING * y for x in range(RING)] for y in range(RING)]
    by_row = shared(by_y.reshape(RING * 32, 2 * W), along_x).reshape(RING, RING, 32, 2 * W)

    c_high, c_low = pl.pallas_call(
        prepare_kernel,
        out_shape=[shape((2, W, 2 * W), BF16)] * 2,
        grid_spec=pltpu.PrefetchScalarGridSpec(
            num_scalar_prefetch=1,
            grid=(2,),
            in_specs=[pl.BlockSpec((16, 1, 32, 2 * W), lambda s, where: (0, s ^ (where[0] // 16), 0, 0))],
            out_specs=[pl.BlockSpec((1, W, 2 * W), lambda s, where: (s, 0, 0))] * 2,
        ),
        compiler_params=PARAMS,
        cost_estimate=cost(0, 8),
        name="prepare",
    )(where, gathered)
    by_row, c_high, c_low = lax.optimization_barrier((by_row, c_high, c_low))

    send_a, send_b0, send_b1, fb_high, fb_low = pl.pallas_call(
        left_kernel,
        out_shape=[shape((HALF, 2 * W), F32)] + [shape((HALF, W), F32)] * 2 + [shape((2, W, HALF), BF16)] * 2,
        in_specs=[SMEM, SMEM] + [VMEM] * 3,
        out_specs=[VMEM] * 5,
        scratch_shapes=[pltpu.VMEM((W, W), BF16)] * 2,
        compiler_params=PARAMS,
        cost_estimate=cost(2, 7),
        name="left",
    )(where, window_live, by_row, hessenberg[:, 0], hessenberg[:, 1])

    every_col = range(GRID_COLS)
    pairs = [((r, c), (r + 1, c)) for r in range(1, 31, 2) for c in every_col]
    got_b1 = swapped(send_b1, [(a, b) for a, b in pairs if a[1] + GRID_COLS >= a[0]])
    got_b0 = swapped(send_b0, [(a, b) for a, b in pairs if a[1] >= a[0]])
    got_a = swapped(send_a, [((r, c), (r + 1, c)) for r in range(0, 32, 2) for c in every_col])

    def middle(first, *parts):
        return pl.pallas_call(
            functools.partial(middle_kernel, first),
            out_shape=[shape((4, HALF, HALF), F32), shape((2, HALF, HALF), F32)] + [shape((HALF, HALF), F32)] * 2,
            in_specs=[SMEM, SMEM] + [VMEM] * 8,
            out_specs=[VMEM] * 4,
            compiler_params=PARAMS,
            cost_estimate=cost(2, 4),
            name="middle",
        )(where, window_live, *parts, fb_high, fb_low, c_high, c_low)

    def exchanged(side, edge0, edge1):
        rows = range(GRID_ROWS)
        side = swapped(side, [((r, c), (r, c + 1)) for r in rows for c in range(0, 16, 2) if r <= c + 17])
        edge0 = swapped(edge0, [((r, c), (r, (c + 1) % 16)) for r in rows for c in range(1, 16, 2) if r <= c + 1])
        edge1 = swapped(edge1, [((r, c), (r, c + 1)) for r in rows for c in range(1, 15, 2) if r <= c + 17])
        return side, edge1, edge0

    def last(first, kept, moved_parts, *done):
        place = lambda i, where: (lax.rem(where[0], 2) ^ (1 if first else 0), 0, 0)
        whole = lambda shape: pl.BlockSpec(shape, lambda i, where: (0,) * len(shape))
        lives = pl.BlockSpec(memory_space=pltpu.SMEM)
        specs = [
            lives,
            whole((4, HALF, HALF)),
            whole((2, HALF, HALF)),
            whole((HALF, HALF)),
            whole((HALF, HALF)),
            whole((2, W, 2 * W)),
            whole((2, W, 2 * W)),
        ]
        return pl.pallas_call(
            functools.partial(last_kernel, first),
            out_shape=shape((W, 2, W), F32),
            grid_spec=pltpu.PrefetchScalarGridSpec(
                num_scalar_prefetch=1,
                grid=(1,),
                in_specs=specs + [pl.BlockSpec(memory_space=pl.ANY)] * len(done),
                out_specs=pl.BlockSpec((HALF, 2, W), place),
            ),
            input_output_aliases={8: 0} if done else {},
            compiler_params=PARAMS,
            cost_estimate=cost(1, 4),
            name="last",
        )(where, window_live, kept, *moved_parts, c_high, c_low, *done)

    kept_a, *ends_a = middle(True, send_a, send_a, got_a, got_a)
    parts_a = exchanged(*ends_a)
    kept_b, *ends_b = middle(False, send_b0, send_b1, got_b0, got_b1)
    parts_b = exchanged(*ends_b)
    out = last(True, kept_a, parts_a)
    return last(False, kept_b, parts_b, out)


def solution(mesh):
    in_specs = (P("row", None, "col"), P("row", "col", None), P("row", "col", None), P())
    out_specs = P("row", None, "col")
    return jax.shard_map(shards, mesh=mesh, in_specs=in_specs, out_specs=out_specs, check_vma=False)
```
